256 devices in a mesh: blk: 64 (over y, z, x_hi), grp: 4 (over x_lo, core).
Axes of the slice: x: 4 (x_hi: 2, x_lo: 2; x = x_hi * 2 + x_lo), y: 4, z: 8, core: 2. Of those that a mesh axis runs over, the one named last changes fastest.
Arguments:
- users: float32 [65536, 256], P(('blk', 'grp')), may hold values from -1.5 to 1.5
- items: float32 [65536, 256], P('blk'), may hold values from -1.5 to 1.5
- noise_users: float32 [2, 65536, 256], P(None, ('blk', 'grp')), may hold values from -6 to 6
- noise_items: float32 [2, 65536, 256], P(None, 'blk'), may hold values from -6 to 6
- tile_index: int32 [2, 2048], P(None, ('blk', 'grp')), may hold values from 0 to 15, as said below
- counts: int32 [2, 256], P(None, ('blk', 'grp')), may hold values from 1 to 8, as said below
- ratings: bfloat16 [2, 2048, 128, 128], P(None, ('blk', 'grp')), may hold values from -6 to 6
- weights: bfloat16 [2, 2048, 128, 128], P(None, ('blk', 'grp')), may hold values from 0 to 2
Outputs:
- users_out: float32 [65536, 256], P(('blk', 'grp'))
- items_out: float32 [65536, 256], P(('blk', 'grp'))
The draws below stay inside these ranges and needn't reach their ends.
Inputs may be any that keep to these rules, and one draw needn't show every extreme that they name: `tile_index`: slot t names user tile row t // 8 of the device's users and item tile column t % 8; the live slots of a device in a stratum name distinct tiles. `counts`: in every stratum some device has 8 live slots.
All inputs are finite; a program needn't handle non-finite values.
Results may differ from the reference program's by a relative error of at most 0.0003.
Values sent between devices are 32-bit elements; how exact they have to be, the bound alone decides.
No kernel may reach another device: no remote copies, remote signals or barrier semaphores. Data moves between devices by JAX's collectives and lax.ppermute only.
A program may use at most 64 MiB of HBM per device.

```python
import math
import jax
import jax.numpy as jnp
from jax import lax

K = 256
TILE = 128
UB = 1024
IB = 1024
STRATA = 2
MAXT = 8
USERS = 65536
ITEMS = 65536
SLOTS = 2048
N_BLK = 64
N_GRP = 4


def draw_tile_index(key, part):
    cells = UB // (N_GRP * TILE) * (IB // TILE)
    devices_all = N_BLK * N_GRP
    keys = jax.random.split(key, STRATA * devices_all)
    rows = jax.vmap(lambda single: jax.random.permutation(single, cells)[:MAXT])(keys)
    return rows.reshape(STRATA, devices_all * MAXT).astype(jnp.int32)


def draw_counts(key, part):
    devices_all = N_BLK * N_GRP
    floor_count = max(1, MAXT * 5 // 8)
    first = jax.random.randint(jax.random.fold_in(key, 11), (STRATA, devices_all), floor_count, MAXT + 1)
    second = jax.random.randint(jax.random.fold_in(key, 12), (STRATA, devices_all), floor_count, MAXT + 1)
    lower = jnp.minimum(first, second)
    chosen = jax.random.randint(jax.random.fold_in(key, 13), (STRATA, 1), 0, devices_all)
    filled = jnp.arange(devices_all)[None, :] == chosen
    return jnp.where(filled, MAXT, lower).astype(jnp.int32)


def draw_weights(key, part):
    shape = (STRATA, N_BLK * N_GRP * MAXT, TILE, TILE)
    keep = jax.random.uniform(jax.random.fold_in(key, 21), shape, jnp.float32) < 0.7
    level = 0.5 + jax.random.uniform(jax.random.fold_in(key, 22), shape, jnp.float32)
    return jnp.where(keep, level, 0.0).astype(jnp.bfloat16)


def steps_of(stream_key, extent, shards, least, largest):
    loudness = 1.0
    for dim, parts in shards:
        draws = jax.random.uniform(jax.random.fold_in(jax.random.fold_in(stream_key, 6), dim), (parts,), jnp.float32, least / len(shards), largest / len(shards))
        loudness = loudness * jnp.repeat(jnp.exp(draws), extent[dim] // parts).reshape((-1,) + (1,) * (len(extent) - 1 - dim))
    return loudness


def centred(rng, shape, scale, bound, shards=(), dtype=jnp.bfloat16):
    drawn = scale * jax.random.normal(rng, shape, jnp.float32)
    if shards:
        drawn = drawn * steps_of(rng, shape, shards, -0.22, 0.18)
    return jnp.clip(drawn, -bound, bound).astype(dtype)


def setup_inputs(seed: int = 0) -> dict:
    key_of = jax.random.split(jax.random.key(seed), 9)
    return {
        "users": centred(key_of[0], (USERS, K), 0.25, 1.5, ((0, 256),), jnp.float32),
        "items": centred(key_of[1], (ITEMS, K), 0.25, 1.5, ((0, 64),), jnp.float32),
        "noise_users": centred(key_of[2], (STRATA, USERS, K), 1.0, 6.0, ((1, 256),), jnp.float32),
        "noise_items": centred(key_of[3], (STRATA, ITEMS, K), 1.0, 6.0, ((1, 64),), jnp.float32),
        "tile_index": draw_tile_index(jax.random.fold_in(key_of[8], 71), 0),
        "counts": draw_counts(jax.random.fold_in(key_of[8], 71), 0),
        "ratings": centred(key_of[6], (STRATA, SLOTS, TILE, TILE), 1.0, 6.0, ((1, 256),)),
        "weights": draw_weights(jax.random.fold_in(key_of[8], 71), 0),
    }


STEP_SIZE = 0.001
LIKELIHOOD = 20.0
NOISE_SCALE = math.sqrt(0.002)
HIGHEST = lax.Precision.HIGHEST

def slot_terms(user_rows, item_block, slot_index, live_slots, rating_tiles, weight_tiles):
    tile = rating_tiles.shape[-1]
    rank = user_rows.shape[1]
    user_tiles = user_rows.shape[0] // tile
    item_tiles = item_block.shape[0] // tile
    tile_row = slot_index // item_tiles
    tile_col = slot_index % item_tiles
    user_table = user_rows.reshape(user_tiles, tile, rank)
    item_table = item_block.reshape(item_tiles, tile, rank)
    user_part = jnp.take(user_table, tile_row, axis=0)
    item_part = jnp.take(item_table, tile_col, axis=0)
    predicted = jnp.einsum('mik,mjk->mij', user_part, item_part, precision=HIGHEST)
    errors = live_slots[:, None, None] * weight_tiles.astype(jnp.float32) * (rating_tiles.astype(jnp.float32) - predicted)
    user_grads = jnp.einsum('mij,mjk->mik', errors, item_part, precision=HIGHEST)
    item_grads = jnp.einsum('mij,mik->mjk', errors, user_part, precision=HIGHEST)
    pick_user = (tile_row[:, None] == jnp.arange(user_tiles)[None, :]).astype(jnp.float32)
    pick_item = (tile_col[:, None] == jnp.arange(item_tiles)[None, :]).astype(jnp.float32)
    grad_users = jnp.einsum('mq,mik->qik', pick_user, user_grads, precision=HIGHEST).reshape(user_tiles * tile, rank)
    grad_items = jnp.einsum('mq,mjk->qjk', pick_item, item_grads, precision=HIGHEST).reshape(item_tiles * tile, rank)
    return (grad_users, grad_items)

def reference(users, items, noise_users, noise_items, tile_index, counts, ratings, weights):
    rank = users.shape[1]
    quarter = UB // N_GRP
    user_now = users
    position = items
    for stratum in range(STRATA):
        user_four = user_now.reshape(N_BLK, N_GRP, quarter, rank)
        blocks = position.reshape(N_BLK, IB, rank)
        slot_ids = tile_index[stratum].reshape(N_BLK, N_GRP, MAXT)
        live_counts = counts[stratum].reshape(N_BLK, N_GRP)
        rating_all = ratings[stratum].reshape(N_BLK, N_GRP, MAXT, TILE, TILE)
        weight_all = weights[stratum].reshape(N_BLK, N_GRP, MAXT, TILE, TILE)

        def one_block(inputs):
            user_block, item_block, block_ids, block_counts, block_ratings, block_weights = inputs

            def member(member_users, member_ids, member_count, member_ratings, member_weights):
                live_slots = (jnp.arange(MAXT) < member_count).astype(jnp.float32)
                return slot_terms(member_users, item_block, member_ids, live_slots, member_ratings, member_weights)
            grad_users, grad_items = jax.vmap(member)(user_block, block_ids, block_counts, block_ratings, block_weights)
            return (grad_users, lax.optimization_barrier(jnp.sum(grad_items, axis=0)))
        grad_users, grad_items = lax.map(one_block, (user_four, blocks, slot_ids, live_counts, rating_all, weight_all))
        grad_users = grad_users.reshape(USERS, rank)
        grad_items = grad_items.reshape(ITEMS, rank)
        user_now = user_now + STEP_SIZE * (LIKELIHOOD * grad_users - user_now) + NOISE_SCALE * noise_users[stratum]
        position = position + STEP_SIZE * (LIKELIHOOD * grad_items - position) + NOISE_SCALE * noise_items[stratum]
        position = jnp.roll(position, IB, axis=0)
    return (user_now, position)
```

```python
import functools
import math

import jax
import jax.numpy as jnp
from jax import lax
from jax.experimental import pallas as pl
from jax.experimental.pallas import tpu as pltpu
from jax.sharding import PartitionSpec as P

STEP_SIZE = 0.001
LIKELIHOOD = 20.0
NOISE_SCALE = math.sqrt(0.002)
GAIN = STEP_SIZE * LIKELIHOOD
AXES = ("blk", "grp")
TILE = 128
CHUNKS = 2
VMEM_LIMIT = 16 * 1024 * 1024

NN = (((1,), (0,)), ((), ()))
NT = (((1,), (1,)), ((), ()))
TN = (((0,), (0,)), ((), ()))


def halves(value):
    high = value.astype(jnp.bfloat16)
    low = (value - high.astype(jnp.float32)).astype(jnp.bfloat16)
    return high, low


def product(left, right, dims):
    dot = functools.partial(
        lax.dot_general, dimension_numbers=dims, preferred_element_type=jnp.float32
    )
    return dot(left[0], right[0]) + (dot(left[0], right[1]) + dot(left[1], right[0]))


def spread(index_ref, count_ref, stratum, rating_ref, weight_ref, rating_out, weight_out):
    rating_out[...] = jnp.zeros_like(rating_out)
    weight_out[...] = jnp.zeros_like(weight_out)
    columns = rating_out.shape[0]
    for slot in range(rating_ref.shape[1]):

        @pl.when(slot < count_ref[stratum, 0])
        def _(slot=slot):
            tile = index_ref[stratum, slot]
            column = lax.rem(tile, columns)
            row = pl.multiple_of(lax.div(tile, columns) * TILE, TILE)
            rating_out[column, pl.ds(row, TILE), :] = rating_ref[0, slot]
            weight_out[column, pl.ds(row, TILE), :] = weight_ref[0, slot]


def tile_errors(user_halves, item_halves, rating, weight):
    predicted = product(user_halves, item_halves, NT)
    return halves(weight.astype(jnp.float32) * (rating.astype(jnp.float32) - predicted))


def item_rows(items_ref, column):
    return items_ref[pl.ds(pl.multiple_of(column * TILE, TILE), TILE), :]


def call(body, outs, operands, cost):
    specs = []
    for array, block, index in operands:
        if index is None:
            specs.append(pl.BlockSpec(memory_space=pltpu.SMEM))
        else:
            specs.append(pl.BlockSpec(block, functools.partial(lambda step, at: at, at=index)))
    out_specs = [
        pl.BlockSpec(shape, functools.partial(lambda step, n: (0,) * n, n=len(shape)))
        for shape, _ in outs
    ]
    return pl.pallas_call(
        body,
        grid=(1,),
        in_specs=specs,
        out_specs=out_specs,
        out_shape=[jax.ShapeDtypeStruct(shape, dtype) for shape, dtype in outs],
        compiler_params=pltpu.CompilerParams(vmem_limit_bytes=VMEM_LIMIT),
        cost_estimate=pl.CostEstimate(flops=cost, bytes_accessed=1 << 20, transcendentals=0),
    )(*[array for array, _, _ in operands])


def whole(array):
    return (array, array.shape, (0,) * array.ndim)


def scalars(array):
    return (array, None, None)


def of_stratum(array, stratum):
    return (array, (1,) + array.shape[1:], (stratum,) + (0,) * (array.ndim - 1))


def body(users, items, noise_users, noise_items, tile_index, counts, ratings, weights):
    f32, bf16 = jnp.float32, jnp.bfloat16
    n_blk, n_grp = lax.axis_size("blk"), lax.axis_size("grp")
    owned, rank = users.shape
    columns = items.shape[0] // TILE
    per_quarter = columns // n_grp
    quarter = per_quarter * TILE
    per_chunk = per_quarter // CHUNKS
    chunk = per_chunk * TILE
    member = lax.axis_index("grp")
    place = member.astype(jnp.int32).reshape(1)

    def swap(value, other):
        pairs = [
            (b * n_grp + g, b * n_grp + (g ^ other)) for b in range(n_blk) for g in range(n_grp)
        ]
        return lax.ppermute(value, AXES, pairs)

    def onward(value):
        pairs = [
            (b * n_grp + g, (b + 1) % n_blk * n_grp + (g ^ 2))
            for b in range(n_blk)
            for g in range(n_grp)
        ]
        return lax.ppermute(value, AXES, pairs)

    dense = (columns, owned, TILE)
    piece = (chunk, rank)

    def piece_grads(user_halves, items_ref, rating_ref, weight_ref, start, outs, user_total):
        for k in range(CHUNKS):
            for t in range(per_chunk):
                column = start + k * per_chunk + t
                item_halves = halves(item_rows(items_ref, column))
                errors = tile_errors(user_halves, item_halves, rating_ref[column], weight_ref[column])
                if outs is not None:
                    outs[k][t * TILE : (t + 1) * TILE, :] = product(errors, user_halves, TN)
                if user_total is not None:
                    user_total = user_total + product(errors, item_halves, NN)
        return user_total

    def first(place_ref, index_ref, count_ref, rating_ref, weight_ref, users_ref, items_ref,
              rating_out, weight_out, *outs):
        spread(index_ref, count_ref, 0, rating_ref, weight_ref, rating_out, weight_out)
        start = (place_ref[0] ^ 1) * per_quarter
        piece_grads(halves(users_ref[...]), items_ref, rating_out, weight_out, start, outs, None)

    unit = 2 * owned * quarter * rank * 3
    rating_0, weight_0, *to_sibling = call(
        first,
        [(dense, bf16)] * 2 + [(piece, f32)] * CHUNKS,
        [scalars(place), scalars(tile_index), scalars(counts), of_stratum(ratings, 0),
         of_stratum(weights, 0), whole(users), whole(items)],
        2 * unit,
    )
    from_sibling = [swap(value, 1) for value in to_sibling]

    def second(place_ref, rating_ref, weight_ref, users_ref, items_ref, *outs):
        start = place_ref[0] * per_quarter
        piece_grads(halves(users_ref[...]), items_ref, rating_ref, weight_ref, start, outs, None)

    mine = call(
        second,
        [(piece, f32)] * CHUNKS,
        [scalars(place), whole(rating_0), whole(weight_0), whole(users), whole(items)],
        2 * unit,
    )
    from_chip = [swap(a + b, 2) for a, b in zip(mine, from_sibling)]

    def third(place_ref, rating_ref, weight_ref, users_ref, items_ref, noise_ref, users_out, *outs):
        user_halves = halves(users_ref[...])
        total = jnp.zeros((owned, rank), f32)
        for flip, target in ((3, outs[:CHUNKS]), (2, outs[CHUNKS:]), (0, None), (1, None)):
            start = (place_ref[0] ^ flip) * per_quarter
            total = piece_grads(
                user_halves, items_ref, rating_ref, weight_ref, start, target, total
            )
        now = users_ref[...]
        users_out[...] = now + STEP_SIZE * (LIKELIHOOD * total - now) + NOISE_SCALE * noise_ref[0]

    users_1, *pieces = call(
        third,
        [(users.shape, f32)] + [(piece, f32)] * (2 * CHUNKS),
        [scalars(place), whole(rating_0), whole(weight_0), whole(users), whole(items),
         of_stratum(noise_users, 0)],
        10 * unit,
    )
    kept = pieces[CHUNKS:]
    from_sibling = [swap(value, 1) for value in pieces[:CHUNKS]]

    def row_chunk(array, flip, k):
        return lax.dynamic_slice_in_dim(array, (member ^ flip) * quarter + k * chunk, chunk, 0)

    def noise_chunk(stratum, flip, k):
        at = (stratum, (member ^ flip) * quarter + k * chunk, 0)
        return lax.dynamic_slice(noise_items, at, (1, chunk, rank))[0]

    ahead = []
    for k in range(CHUNKS):
        rows = row_chunk(items, 2, k)
        base = rows - STEP_SIZE * rows + NOISE_SCALE * noise_chunk(0, 2, k)
        base = lax.optimization_barrier(base + GAIN * (kept[k] + from_sibling[k]))
        ahead.append(onward(base + GAIN * from_chip[k]))

    half = (columns // 2, owned, TILE)

    def layout(place_ref, index_ref, count_ref, rating_ref, weight_ref,
               rating_out, weight_out, rating_send, weight_send):
        spread(index_ref, count_ref, 1, rating_ref, weight_ref, rating_out, weight_out)
        for n, flip in enumerate((1, 3)):
            for t in range(per_quarter):
                column = (place_ref[0] ^ flip) * per_quarter + t
                rating_send[n * per_quarter + t] = rating_out[column].astype(f32)
                weight_send[n * per_quarter + t] = weight_out[column].astype(f32)

    rating_1, weight_1, rating_send, weight_send = call(
        layout,
        [(dense, bf16)] * 2 + [(half, f32)] * 2,
        [scalars(place), scalars(tile_index), scalars(counts), of_stratum(ratings, 1),
         of_stratum(weights, 1)],
        unit,
    )
    rating_s, weight_s, users_s = swap(rating_send, 1), swap(weight_send, 1), swap(users_1, 1)

    def late(k, slot, place_ref, items_ref, users_ref, users_s_ref, rating_ref, weight_ref,
             rating_s_ref, weight_s_ref, *rest):
        own, other = halves(users_ref[...]), halves(users_s_ref[...])
        out = rest[-1]
        for t in range(per_chunk):
            offset = k * per_chunk + t
            column = (place_ref[0] ^ (2 * slot)) * per_quarter + offset
            rows = slice(t * TILE, (t + 1) * TILE)
            now = items_ref[rows, :]
            item_halves = halves(now)
            errors = tile_errors(own, item_halves, rating_ref[column], weight_ref[column])
            total = product(errors, own, TN)
            at = slot * per_quarter + offset
            errors = tile_errors(other, item_halves, rating_s_ref[at], weight_s_ref[at])
            total = total + product(errors, other, TN)
            if slot == 1:
                total = now + STEP_SIZE * (LIKELIHOOD * total - now) + NOISE_SCALE * rest[0][rows, :]
            out[rows, :] = total

    near, far, near_s, far_s, final = [], [], [], [], []
    for k in range(CHUNKS):
        common = [whole(users_1), whole(users_s), whole(rating_1), whole(weight_1),
                  whole(rating_s), whole(weight_s)]
        here = ahead[k]
        there = swap(here, 2)
        [send] = call(
            functools.partial(late, k, 0), [(piece, f32)],
            [scalars(place), whole(here)] + common, 4 * unit // CHUNKS,
        )
        received = swap(send, 2)
        noise = lax.optimization_barrier(noise_chunk(1, 2, k))
        [base] = call(
            functools.partial(late, k, 1), [(piece, f32)],
            [scalars(place), whole(there)] + common + [whole(noise)], 4 * unit // CHUNKS,
        )
        final.append(onward(base + GAIN * received))
        near.append(here)
        far.append(there)
        near_s.append(swap(here, 1))
        far_s.append(swap(there, 1))

    def last(place_ref, rating_ref, weight_ref, users_ref, noise_ref, *rest):
        blocks, users_out = rest[:-1], rest[-1]
        user_halves = halves(users_ref[...])
        total = jnp.zeros((owned, rank), f32)
        for n, flip in enumerate((0, 1, 2, 3)):
            for k in range(CHUNKS):
                for t in range(per_chunk):
                    column = (place_ref[0] ^ flip) * per_quarter + k * per_chunk + t
                    item_halves = halves(blocks[n * CHUNKS + k][t * TILE : (t + 1) * TILE, :])
                    errors = tile_errors(user_halves, item_halves, rating_ref[column], weight_ref[column])
                    total = total + product(errors, item_halves, NN)
        now = users_ref[...]
        users_out[...] = now + STEP_SIZE * (LIKELIHOOD * total - now) + NOISE_SCALE * noise_ref[0]

    [users_out] = call(
        last,
        [(users.shape, f32)],
        [scalars(place), whole(rating_1), whole(weight_1), whole(users_1), of_stratum(noise_users, 1)]
        + [whole(v) for v in near + near_s + far + far_s],
        8 * unit,
    )
    return (users_out, jnp.concatenate(final, 0))


def solution(mesh):
    in_specs = (
        P(("blk", "grp"), None),
        P("blk", None),
        P(None, ("blk", "grp"), None),
        P(None, "blk", None),
        P(None, ("blk", "grp")),
        P(None, ("blk", "grp")),
        P(None, ("blk", "grp"), None, None),
        P(None, ("blk", "grp"), None, None),
    )
    out_specs = (P(("blk", "grp"), None), P(("blk", "grp"), None))
    return jax.shard_map(body, mesh=mesh, in_specs=in_specs, out_specs=out_specs, check_vma=False)
```

```python
import functools
import math

import jax
import jax.numpy as jnp
from jax import lax
from jax.experimental import pallas as pl
from jax.experimental.pallas import tpu as pltpu
from jax.sharding import PartitionSpec as P

STEP_SIZE = 0.001
LIKELIHOOD = 20.0
NOISE_SCALE = math.sqrt(0.002)
GAIN = STEP_SIZE * LIKELIHOOD
AXES = ("blk", "grp")
TILE = 128
CHUNKS = 2
WEIGHT = 8
THIRD = 64
SHORT = 4
MOVE = 64
VMEM_LIMIT = 16 * 1024 * 1024

NN = (((1,), (0,)), ((), ()))
NT = (((1,), (1,)), ((), ()))
TN = (((0,), (0,)), ((), ()))


def halves(value):
    high = value.astype(jnp.bfloat16)
    low = (value - high.astype(jnp.float32)).astype(jnp.bfloat16)
    return high, low


def product(left, right, dims):
    dot = functools.partial(
        lax.dot_general, dimension_numbers=dims, preferred_element_type=jnp.float32
    )
    return dot(left[0], right[0]) + (dot(left[0], right[1]) + dot(left[1], right[0]))


def errors_of(item_halves, user_halves, rating, weight):
    predicted = product(item_halves, user_halves, NT)
    return halves(weight.astype(jnp.float32) * (rating.astype(jnp.float32) - predicted))


def stepped(now, total, noise):
    return now + STEP_SIZE * (LIKELIHOOD * total - now) + NOISE_SCALE * noise


SCALARS = pl.BlockSpec(memory_space=pltpu.SMEM)
LOCAL = pl.BlockSpec(memory_space=pltpu.VMEM)
DISTANT = pl.BlockSpec(memory_space=pltpu.HBM)
AFTER = pl.BlockSpec(memory_space=pl.ANY)


def call(body, outs, operands, cost, scratch=(), after=()):
    unread = len(after)

    def kernel(*refs):
        body(*refs[unread:])

    return pl.pallas_call(
        kernel,
        in_specs=[AFTER] * unread + [spec for spec, _ in operands],
        out_specs=[LOCAL] * len(outs),
        out_shape=[jax.ShapeDtypeStruct(shape, dtype) for shape, dtype in outs],
        scratch_shapes=list(scratch),
        compiler_params=pltpu.CompilerParams(vmem_limit_bytes=VMEM_LIMIT),
        cost_estimate=pl.CostEstimate(
            flops=WEIGHT * cost, bytes_accessed=1 << 18, transcendentals=0
        ),
        name=body.__name__ if hasattr(body, "__name__") else body.func.__name__,
    )(*after, *[held(spec, array) for spec, array in operands])


def held(spec, array):
    return pltpu.with_memory_space_constraint(array, pltpu.HBM) if spec is DISTANT else array


def local(array):
    return (LOCAL, array)


def body(users, items, noise_users, noise_items, tile_index, counts, ratings, weights):
    f32, bf16 = jnp.float32, jnp.bfloat16
    n_blk, n_grp = lax.axis_size("blk"), lax.axis_size("grp")
    owned, rank = users.shape
    slots = ratings.shape[1]
    columns = items.shape[0] // TILE
    per_quarter = columns // n_grp
    quarter = per_quarter * TILE
    chunk = quarter // CHUNKS
    place = (SCALARS, lax.axis_index("grp").astype(jnp.int32).reshape(1))

    def swap(value, other):
        pairs = [
            (b * n_grp + g, b * n_grp + (g ^ other)) for b in range(n_blk) for g in range(n_grp)
        ]
        with jax.named_scope("core_swap" if other == 1 else "chip_swap"):
            return lax.ppermute(value, AXES, pairs)

    def onward(value):
        pairs = [
            (b * n_grp + g, (b + 1) % n_blk * n_grp + (g ^ 2))
            for b in range(n_blk)
            for g in range(n_grp)
        ]
        with jax.named_scope("onward"):
            return lax.ppermute(value, AXES, pairs)

    dense = (columns, owned, TILE)
    piece = (chunk, rank)
    square = (quarter, owned)
    unit = 2 * owned * quarter * rank * 3

    def rows_of(place_ref, flip):
        return pl.ds(pl.multiple_of((place_ref[0] ^ flip) * quarter, quarter), quarter)

    def side_by_side(dense_ref, start):
        return jnp.concatenate([dense_ref[start + t] for t in range(per_quarter)], 1)

    def quarter_terms(place_ref, flip, rating_ref, weight_ref, users_ref, items_ref, high_ref, low_ref):
        start = (place_ref[0] ^ flip) * per_quarter
        user_halves = halves(users_ref[...])
        item_halves = halves(items_ref[rows_of(place_ref, flip), :])
        rating = side_by_side(rating_ref, start).astype(f32).T
        weight = side_by_side(weight_ref, start).astype(f32).T
        errors = errors_of(item_halves, user_halves, rating, weight)
        high_ref[...], low_ref[...] = errors
        return product(errors, user_halves, NN)

    def put(value, outs):
        for k, out in enumerate(outs):
            out[...] = value[k * chunk : (k + 1) * chunk, :]

    def fetch(pairs, sems):
        copies = [pltpu.make_async_copy(a, b, sems.at[n]) for n, (a, b) in enumerate(pairs)]
        for copy in copies:
            copy.start()
        return copies

    live = counts.reshape(-1)
    tables = [(DISTANT, tile_index), (DISTANT, live), (DISTANT, ratings), (DISTANT, weights)]
    landing = [
        pltpu.SMEM(tile_index.shape, jnp.int32),
        pltpu.SMEM(live.shape, jnp.int32),
        pltpu.VMEM(ratings.shape[1:], bf16),
        pltpu.VMEM(weights.shape[1:], bf16),
    ]

    def first(place_ref, index_hbm, count_hbm, rating_hbm, weight_hbm, users_hbm, items_hbm,
              rating_out, weight_out, users_out, items_out, high_out, low_out, *rest):
        outs, (index_ref, count_ref, rating_in, weight_in, sems) = rest[:CHUNKS], rest[CHUNKS:]
        copies = fetch(
            [(index_hbm, index_ref), (count_hbm, count_ref),
             (rating_hbm.at[0], rating_in), (weight_hbm.at[0], weight_in),
             (users_hbm, users_out), (items_hbm, items_out)],
            sems,
        )
        rating_out[...] = jnp.zeros_like(rating_out)
        weight_out[...] = jnp.zeros_like(weight_out)
        for copy in copies[:4]:
            copy.wait()
        for slot in range(slots):

            @pl.when(slot < count_ref[0])
            def _(slot=slot):
                tile = index_ref[0, slot]
                column = lax.rem(tile, columns)
                row = pl.multiple_of(lax.div(tile, columns) * TILE, TILE)
                rating_out[column, pl.ds(row, TILE), :] = rating_in[slot]
                weight_out[column, pl.ds(row, TILE), :] = weight_in[slot]

        copies[4].wait()
        copies[5].wait()
        put(quarter_terms(place_ref, 1, rating_out, weight_out, users_out, items_out,
                          high_out, low_out), outs)

    rating_0, weight_0, users_0, items_0, *rest = call(
        first,
        [(dense, bf16)] * 2 + [(users.shape, f32), (items.shape, f32)] + [(square, bf16)] * 2
        + [(piece, f32)] * CHUNKS,
        [place] + tables + [(DISTANT, users), (DISTANT, items)],
        2 * unit,
        landing + [pltpu.SemaphoreType.DMA((6,))],
    )
    errors_1, to_sibling = rest[:2], rest[2:]
    from_sibling = [swap(value, 1) for value in to_sibling]
    stage_0 = [local(rating_0), local(weight_0), local(users_0), local(items_0)]

    def second(place_ref, rating_ref, weight_ref, users_ref, items_ref, high_out, low_out, *outs):
        put(quarter_terms(place_ref, 0, rating_ref, weight_ref, users_ref, items_ref,
                          high_out, low_out), outs)

    high_0, low_0, *mine = call(
        second, [(square, bf16)] * 2 + [(piece, f32)] * CHUNKS, [place] + stage_0, 2 * unit
    )
    errors_0 = [high_0, low_0]

    def join(a_ref, b_ref, out):
        out[...] = a_ref[...] + b_ref[...]

    def add_scaled(base_ref, *rest):
        total = rest[0][...]
        for ref in rest[1:-1]:
            total = total + ref[...]
        rest[-1][...] = base_ref[...] + GAIN * total

    to_chip = []
    for k in range(CHUNKS):
        [value] = call(join, [(piece, f32)], [local(mine[k]), local(from_sibling[k])], 1, after=to_chip[-1:])
        to_chip.append(value)
    from_chip = [swap(value, 2) for value in to_chip]

    def third(place_ref, rating_ref, weight_ref, users_ref, items_ref, noise_hbm,
              high_3, low_3, high_2, low_2, *rest):
        outs, bases, (noise, sems) = rest[:CHUNKS], rest[CHUNKS : 2 * CHUNKS], rest[2 * CHUNKS :]
        [copy] = fetch([(noise_hbm.at[0, rows_of(place_ref, 2), :], noise)], sems)
        args = (rating_ref, weight_ref, users_ref, items_ref)
        put(quarter_terms(place_ref, 3, *args, high_3, low_3), outs)
        total = quarter_terms(place_ref, 2, *args, high_2, low_2)
        copy.wait()
        put(stepped(items_ref[rows_of(place_ref, 2), :], total, noise[...]), bases)

    *rest, = call(
        third,
        [(square, bf16)] * 4 + [(piece, f32)] * (2 * CHUNKS),
        [place] + stage_0 + [(DISTANT, noise_items)],
        THIRD * unit,
        [pltpu.VMEM((quarter, rank), f32), pltpu.SemaphoreType.DMA((1,))],
        after=to_chip,
    )
    errors_3, errors_2, to_sibling, base = rest[:2], rest[2:4], rest[4 : 4 + CHUNKS], rest[4 + CHUNKS :]
    from_sibling = [swap(value, 1) for value in to_sibling]

    def user_step(place_ref, users_ref, items_ref, noise_hbm, *rest):
        errors, (users_out, noise, sems) = rest[:-3], rest[-3:]
        [copy] = fetch([(noise_hbm.at[0], noise)], sems)
        total = jnp.zeros((owned, rank), f32)
        for flip in range(n_grp):
            item_halves = halves(items_ref[rows_of(place_ref, flip), :])
            kept = (errors[2 * flip][...], errors[2 * flip + 1][...])
            total = total + product(kept, item_halves, TN)
        copy.wait()
        users_out[...] = stepped(users_ref[...], total, noise[...])

    [users_1] = call(
        user_step,
        [(users.shape, f32)],
        [place, local(users_0), local(items_0), (DISTANT, noise_users)]
        + [local(v) for v in errors_0 + errors_1 + errors_2 + errors_3],
        SHORT * unit,
        [pltpu.VMEM(users.shape, f32), pltpu.SemaphoreType.DMA((1,))],
        after=to_sibling,
    )
    users_s = swap(users_1, 1)

    flat = (columns * TILE, owned)
    half = (columns * TILE // 2, owned)

    def layout(place_ref, index_hbm, count_hbm, rating_hbm, weight_hbm, noise_hbm,
               rating_out, weight_out, rating_send, weight_send, noise_out,
               index_ref, count_ref, rating_in, weight_in, sems):
        copies = fetch(
            [(index_hbm, index_ref), (count_hbm, count_ref),
             (rating_hbm.at[1], rating_in), (weight_hbm.at[1], weight_in),
             (noise_hbm.at[1, rows_of(place_ref, 2), :], noise_out)],
            sems,
        )
        rating_out[...] = jnp.zeros_like(rating_out)
        weight_out[...] = jnp.zeros_like(weight_out)
        for copy in copies[:4]:
            copy.wait()
        for slot in range(slots):

            @pl.when(slot < count_ref[1])
            def _(slot=slot):
                tile = index_ref[1, slot]
                at = pl.ds(pl.multiple_of(lax.rem(tile, columns) * TILE, TILE), TILE)
                turned = (rating_in[slot].astype(f32).T, weight_in[slot].astype(f32).T)
                for row in range(owned // TILE):

                    @pl.when(lax.div(tile, columns) == row)
                    def _(row=row):
                        across = slice(row * TILE, (row + 1) * TILE)
                        rating_out[at, across] = turned[0]
                        weight_out[at, across] = turned[1]

        for n, flip in enumerate((1, 3)):
            rows = slice(n * quarter, (n + 1) * quarter)
            rating_send[rows, :] = rating_out[rows_of(place_ref, flip), :]
            weight_send[rows, :] = weight_out[rows_of(place_ref, flip), :]
        copies[4].wait()

    rating_1, weight_1, rating_send, weight_send, noise_1 = call(
        layout,
        [(flat, f32)] * 2 + [(half, f32)] * 2 + [((quarter, rank), f32)],
        [place] + tables + [(DISTANT, noise_items)],
        SHORT * unit,
        landing + [pltpu.SemaphoreType.DMA((5,))],
        after=[users_1],
    )
    rating_s, weight_s = swap(rating_send, 1), swap(weight_send, 1)

    moved = []
    for k in range(CHUNKS):
        [value] = call(
            add_scaled, [(piece, f32)],
            [local(v) for v in (base[k], from_sibling[k], from_chip[k])], MOVE * unit,
            after=[rating_send, *moved[-1:]],
        )
        moved.append(value)
    ahead = [onward(value) for value in moved]

    def late(k, slot, place_ref, items_ref, users_ref, users_s_ref, rating_ref, weight_ref,
             rating_s_ref, weight_s_ref, *rest):
        high_out, low_out, copy_out, out = rest[-4:]
        own, other = halves(users_ref[...]), halves(users_s_ref[...])
        now = items_ref[...]
        copy_out[...] = now
        item_halves = halves(now)
        at = pl.ds(pl.multiple_of((place_ref[0] ^ (2 * slot)) * quarter + k * chunk, chunk), chunk)
        errors = errors_of(item_halves, own, rating_ref[at, :], weight_ref[at, :])
        high_out[...], low_out[...] = errors
        total = product(errors, own, NN)
        at = slice(slot * quarter + k * chunk, slot * quarter + (k + 1) * chunk)
        errors = errors_of(item_halves, other, rating_s_ref[at, :], weight_s_ref[at, :])
        total = total + product(errors, other, NN)
        if slot == 1:
            total = stepped(now, total, rest[0][k * chunk : (k + 1) * chunk, :])
        out[...] = total

    common = [local(v) for v in (users_1, users_s, rating_1, weight_1, rating_s, weight_s)]
    errors_shape = (chunk, owned)
    late_outs = [(errors_shape, bf16)] * 2 + [(piece, f32)] * 2
    here = ahead
    there = [swap(value, 2) for value in here]
    errors_here, here_copy, sent = [], [], []
    for k in range(CHUNKS):
        high, low, rows, value = call(
            functools.partial(late, k, 0), late_outs, [place, local(here[k])] + common,
            4 * unit // CHUNKS, after=sent[-1:],
        )
        errors_here.append((high, low))
        here_copy.append(rows)
        sent.append(value)
    received = [swap(value, 2) for value in sent]
    errors_there, there_copy, finished = [], [], []
    for k in range(CHUNKS):
        high, low, rows, step = call(
            functools.partial(late, k, 1), late_outs,
            [place, local(there[k])] + common + [local(noise_1)], 4 * unit // CHUNKS,
            after=[sent[-1], *finished[-1:]],
        )
        [value] = call(add_scaled, [(piece, f32)], [local(step), local(received[k])], 1)
        errors_there.append((high, low))
        there_copy.append(rows)
        finished.append(value)
    final = [onward(value) for value in finished]
    here_s = [swap(value, 1) for value in here_copy]
    there_s = [swap(value, 1) for value in there_copy]

    def last(place_ref, rating_ref, weight_ref, users_ref, noise_hbm, *rest):
        known, blocks = rest[: 6 * CHUNKS], rest[6 * CHUNKS : 8 * CHUNKS]
        users_out, token, noise, sems = rest[8 * CHUNKS :]
        token[...] = jnp.zeros_like(token)
        [copy] = fetch([(noise_hbm.at[1], noise)], sems)
        user_halves = halves(users_ref[...])
        total = jnp.zeros((owned, rank), f32)
        for n in range(2 * CHUNKS):
            errors = (known[3 * n][...], known[3 * n + 1][...])
            total = total + product(errors, halves(known[3 * n + 2][...]), TN)
        for n, block in enumerate(blocks):
            flip, k = (1, 3)[n // CHUNKS], n % CHUNKS
            at = pl.ds(pl.multiple_of((place_ref[0] ^ flip) * quarter + k * chunk, chunk), chunk)
            item_halves = halves(block[...])
            errors = errors_of(item_halves, user_halves, rating_ref[at, :], weight_ref[at, :])
            total = total + product(errors, item_halves, TN)
        copy.wait()
        users_out[...] = stepped(users_ref[...], total, noise[...])

    known = [
        local(v)
        for errors, rows in zip(errors_here + errors_there, here + there)
        for v in (*errors, rows)
    ]
    users_out, token = call(
        last,
        [(users.shape, f32), ((8, 128), f32)],
        [place, local(rating_1), local(weight_1), local(users_1), (DISTANT, noise_users)]
        + known + [local(v) for v in here_s + there_s],
        6 * unit,
        [pltpu.VMEM(users.shape, f32), pltpu.SemaphoreType.DMA((1,))],
        after=finished,
    )

    def gather(*refs):
        for k in range(CHUNKS):
            refs[-1][k * chunk : (k + 1) * chunk, :] = refs[k][...]

    [items_out] = call(
        gather, [((quarter, rank), f32)], [local(v) for v in final], 1, after=[token]
    )
    return (users_out, items_out)


def solution(mesh):
    in_specs = (
        P(("blk", "grp"), None),
        P("blk", None),
        P(None, ("blk", "grp"), None),
        P(None, "blk", None),
        P(None, ("blk", "grp")),
        P(None, ("blk", "grp")),
        P(None, ("blk", "grp"), None, None),
        P(None, ("blk", "grp"), None, None),
    )
    out_specs = (P(("blk", "grp"), None), P(("blk", "grp"), None))
    return jax.shard_map(body, mesh=mesh, in_specs=in_specs, out_specs=out_specs, check_vma=False)
```

```python
import functools
import math

import jax
import jax.numpy as jnp
from jax import lax
from jax.experimental import pallas as pl
from jax.experimental.pallas import tpu as pltpu
from jax.sharding import PartitionSpec as P

STEP_SIZE = 0.001
LIKELIHOOD = 20.0
NOISE_SCALE = math.sqrt(0.002)
GAIN = STEP_SIZE * LIKELIHOOD
AXES = ("blk", "grp")
TILE = 128
CHUNKS = 2
WEIGHT = 8
THIRD = 64
SHORT = 4
MOVE = 64
FAR = (2, 8)
LAST = 6
FIN = 8
VMEM_LIMIT = 16 * 1024 * 1024

NN = (((1,), (0,)), ((), ()))
NT = (((1,), (1,)), ((), ()))
TN = (((0,), (0,)), ((), ()))


def halves(value):
    high = value.astype(jnp.bfloat16)
    low = (value - high.astype(jnp.float32)).astype(jnp.bfloat16)
    return high, low


def product(left, right, dims):
    dot = functools.partial(
        lax.dot_general, dimension_numbers=dims, preferred_element_type=jnp.float32
    )
    return dot(left[0], right[0]) + (dot(left[0], right[1]) + dot(left[1], right[0]))


def errors_of(item_halves, user_halves, rating, weight):
    predicted = product(item_halves, user_halves, NT)
    return halves(weight.astype(jnp.float32) * (rating.astype(jnp.float32) - predicted))


def stepped(now, total, noise):
    return now + STEP_SIZE * (LIKELIHOOD * total - now) + NOISE_SCALE * noise


SCALARS = pl.BlockSpec(memory_space=pltpu.SMEM)
LOCAL = pl.BlockSpec(memory_space=pltpu.VMEM)
DISTANT = pl.BlockSpec(memory_space=pltpu.HBM)
AFTER = pl.BlockSpec(memory_space=pl.ANY)


def call(body, outs, operands, cost, scratch=(), after=()):
    unread = len(after)

    def kernel(*refs):
        body(*refs[unread:])

    return pl.pallas_call(
        kernel,
        in_specs=[AFTER] * unread + [spec for spec, _ in operands],
        out_specs=[LOCAL] * len(outs),
        out_shape=[jax.ShapeDtypeStruct(shape, dtype) for shape, dtype in outs],
        scratch_shapes=list(scratch),
        compiler_params=pltpu.CompilerParams(vmem_limit_bytes=VMEM_LIMIT),
        cost_estimate=pl.CostEstimate(
            flops=WEIGHT * cost, bytes_accessed=1 << 18, transcendentals=0
        ),
        name=body.__name__ if hasattr(body, "__name__") else body.func.__name__,
    )(*after, *[held(spec, array) for spec, array in operands])


def held(spec, array):
    return pltpu.with_memory_space_constraint(array, pltpu.HBM) if spec is DISTANT else array


def local(array):
    return (LOCAL, array)


def body(users, items, noise_users, noise_items, tile_index, counts, ratings, weights):
    f32, bf16 = jnp.float32, jnp.bfloat16
    n_blk, n_grp = lax.axis_size("blk"), lax.axis_size("grp")
    owned, rank = users.shape
    slots = ratings.shape[1]
    columns = items.shape[0] // TILE
    per_quarter = columns // n_grp
    quarter = per_quarter * TILE
    chunk = quarter // CHUNKS
    place = (SCALARS, lax.axis_index("grp").astype(jnp.int32).reshape(1))

    def swap(value, other):
        pairs = [
            (b * n_grp + g, b * n_grp + (g ^ other)) for b in range(n_blk) for g in range(n_grp)
        ]
        with jax.named_scope("core_swap" if other == 1 else "chip_swap"):
            return lax.ppermute(value, AXES, pairs)

    def onward(value):
        pairs = [
            (b * n_grp + g, (b + 1) % n_blk * n_grp + (g ^ 2))
            for b in range(n_blk)
            for g in range(n_grp)
        ]
        with jax.named_scope("onward"):
            return lax.ppermute(value, AXES, pairs)

    dense = (columns, owned, TILE)
    piece = (chunk, rank)
    square = (quarter, owned)
    unit = 2 * owned * quarter * rank * 3

    def rows_of(place_ref, flip):
        return pl.ds(pl.multiple_of((place_ref[0] ^ flip) * quarter, quarter), quarter)

    def side_by_side(dense_ref, start):
        return jnp.concatenate([dense_ref[start + t] for t in range(per_quarter)], 1)

    def quarter_terms(place_ref, flip, rating_ref, weight_ref, users_ref, items_ref, high_ref, low_ref):
        start = (place_ref[0] ^ flip) * per_quarter
        user_halves = halves(users_ref[...])
        item_halves = halves(items_ref[rows_of(place_ref, flip), :])
        rating = side_by_side(rating_ref, start).astype(f32).T
        weight = side_by_side(weight_ref, start).astype(f32).T
        errors = errors_of(item_halves, user_halves, rating, weight)
        high_ref[...], low_ref[...] = errors
        return product(errors, user_halves, NN)

    def put(value, outs):
        for k, out in enumerate(outs):
            out[...] = value[k * chunk : (k + 1) * chunk, :]

    def fetch(pairs, sems):
        copies = [pltpu.make_async_copy(a, b, sems.at[n]) for n, (a, b) in enumerate(pairs)]
        for copy in copies:
            copy.start()
        return copies

    live = counts.reshape(-1)
    tables = [(DISTANT, tile_index), (DISTANT, live), (DISTANT, ratings), (DISTANT, weights)]
    landing = [
        pltpu.SMEM(tile_index.shape, jnp.int32),
        pltpu.SMEM(live.shape, jnp.int32),
        pltpu.VMEM(ratings.shape[1:], bf16),
        pltpu.VMEM(weights.shape[1:], bf16),
    ]

    def first(place_ref, index_hbm, count_hbm, rating_hbm, weight_hbm, users_hbm, items_hbm,
              rating_out, weight_out, users_out, items_out, high_out, low_out, *rest):
        outs, (index_ref, count_ref, rating_in, weight_in, sems) = rest[:CHUNKS], rest[CHUNKS:]
        copies = fetch(
            [(index_hbm, index_ref), (count_hbm, count_ref),
             (rating_hbm.at[0], rating_in), (weight_hbm.at[0], weight_in),
             (users_hbm, users_out), (items_hbm, items_out)],
            sems,
        )
        rating_out[...] = jnp.zeros_like(rating_out)
        weight_out[...] = jnp.zeros_like(weight_out)
        for copy in copies[:4]:
            copy.wait()
        for slot in range(slots):

            @pl.when(slot < count_ref[0])
            def _(slot=slot):
                tile = index_ref[0, slot]
                column = lax.rem(tile, columns)
                row = pl.multiple_of(lax.div(tile, columns) * TILE, TILE)
                rating_out[column, pl.ds(row, TILE), :] = rating_in[slot]
                weight_out[column, pl.ds(row, TILE), :] = weight_in[slot]

        copies[4].wait()
        copies[5].wait()
        put(quarter_terms(place_ref, 1, rating_out, weight_out, users_out, items_out,
                          high_out, low_out), outs)

    rating_0, weight_0, users_0, items_0, *rest = call(
        first,
        [(dense, bf16)] * 2 + [(users.shape, f32), (items.shape, f32)] + [(square, bf16)] * 2
        + [(piece, f32)] * CHUNKS,
        [place] + tables + [(DISTANT, users), (DISTANT, items)],
        2 * unit,
        landing + [pltpu.SemaphoreType.DMA((6,))],
    )
    errors_1, to_sibling = rest[:2], rest[2:]
    from_sibling = [swap(value, 1) for value in to_sibling]
    stage_0 = [local(rating_0), local(weight_0), local(users_0), local(items_0)]

    def second(place_ref, rating_ref, weight_ref, users_ref, items_ref, high_out, low_out, *outs):
        put(quarter_terms(place_ref, 0, rating_ref, weight_ref, users_ref, items_ref,
                          high_out, low_out), outs)

    high_0, low_0, *mine = call(
        second, [(square, bf16)] * 2 + [(piece, f32)] * CHUNKS, [place] + stage_0, 2 * unit
    )
    errors_0 = [high_0, low_0]

    def join(a_ref, b_ref, out):
        out[...] = a_ref[...] + b_ref[...]

    def add_scaled(base_ref, *rest):
        total = rest[0][...]
        for ref in rest[1:-1]:
            total = total + ref[...]
        rest[-1][...] = base_ref[...] + GAIN * total

    to_chip = []
    for k in range(CHUNKS):
        [value] = call(join, [(piece, f32)], [local(mine[k]), local(from_sibling[k])], 1, after=to_chip[-1:])
        to_chip.append(value)
    from_chip = [swap(value, 2) for value in to_chip]

    def third(place_ref, rating_ref, weight_ref, users_ref, items_ref, noise_hbm,
              rating_hbm, weight_hbm, noise_users_hbm,
              rating_out, weight_out, noise_out, noise_users_out,
              high_3, low_3, high_2, low_2, *rest):
        outs, bases, (noise, sems) = rest[:CHUNKS], rest[CHUNKS : 2 * CHUNKS], rest[2 * CHUNKS :]
        copies = fetch(
            [(noise_hbm.at[0, rows_of(place_ref, 2), :], noise),
             (rating_hbm.at[1], rating_out), (weight_hbm.at[1], weight_out),
             (noise_hbm.at[1, rows_of(place_ref, 2), :], noise_out),
             (noise_users_hbm.at[0], noise_users_out)],
            sems,
        )
        args = (rating_ref, weight_ref, users_ref, items_ref)
        put(quarter_terms(place_ref, 3, *args, high_3, low_3), outs)
        total = quarter_terms(place_ref, 2, *args, high_2, low_2)
        for copy in copies:
            copy.wait()
        put(stepped(items_ref[rows_of(place_ref, 2), :], total, noise[...]), bases)

    tiles_shape = (ratings.shape[1:], bf16)
    rating_in, weight_in, noise_1, noise_users_0, *rest = call(
        third,
        [tiles_shape] * 2 + [((quarter, rank), f32), (users.shape, f32)]
        + [(square, bf16)] * 4 + [(piece, f32)] * (2 * CHUNKS),
        [place] + stage_0
        + [(DISTANT, v) for v in (noise_items, ratings, weights, noise_users)],
        THIRD * unit,
        [pltpu.VMEM((quarter, rank), f32), pltpu.SemaphoreType.DMA((5,))],
        after=to_chip,
    )
    errors_3, errors_2, to_sibling, base = rest[:2], rest[2:4], rest[4 : 4 + CHUNKS], rest[4 + CHUNKS :]
    from_sibling = [swap(value, 1) for value in to_sibling]

    flat = (columns * TILE, owned)
    half = (columns * TILE // 2, owned)

    def layout(place_ref, index_hbm, count_hbm, rating_ref, weight_ref,
               rating_out, weight_out, rating_send, weight_send, index_ref, count_ref, sems):
        copies = fetch([(index_hbm, index_ref), (count_hbm, count_ref)], sems)
        rating_out[...] = jnp.zeros_like(rating_out)
        weight_out[...] = jnp.zeros_like(weight_out)
        for copy in copies:
            copy.wait()
        for slot in range(slots):

            @pl.when(slot < count_ref[1])
            def _(slot=slot):
                tile = index_ref[1, slot]
                at = pl.ds(pl.multiple_of(lax.rem(tile, columns) * TILE, TILE), TILE)
                turned = (rating_ref[slot].astype(f32).T, weight_ref[slot].astype(f32).T)
                for row in range(owned // TILE):

                    @pl.when(lax.div(tile, columns) == row)
                    def _(row=row):
                        across = slice(row * TILE, (row + 1) * TILE)
                        rating_out[at, across] = turned[0]
                        weight_out[at, across] = turned[1]

        for n, flip in enumerate((1, 3)):
            rows = slice(n * quarter, (n + 1) * quarter)
            rating_send[rows, :] = rating_out[rows_of(place_ref, flip), :]
            weight_send[rows, :] = weight_out[rows_of(place_ref, flip), :]
    rating_1, weight_1, rating_send, weight_send = call(
        layout,
        [(flat, f32)] * 2 + [(half, f32)] * 2,
        [place] + tables[:2] + [local(rating_in), local(weight_in)],
        SHORT * unit,
        landing[:2] + [pltpu.SemaphoreType.DMA((2,))],
        after=to_sibling,
    )
    rating_s, weight_s = swap(rating_send, 1), swap(weight_send, 1)

    def move(k, after):
        terms = [local(v) for v in (base[k], from_sibling[k], from_chip[k])]
        return call(add_scaled, [(piece, f32)], terms, MOVE * unit, after=after)

    moved = move(0, [rating_send])

    def user_step(place_ref, users_ref, items_ref, noise_ref, *rest):
        errors, users_out = rest[:-1], rest[-1]
        total = jnp.zeros((owned, rank), f32)
        for flip in range(n_grp):
            item_halves = halves(items_ref[rows_of(place_ref, flip), :])
            kept = (errors[2 * flip][...], errors[2 * flip + 1][...])
            total = total + product(kept, item_halves, TN)
        users_out[...] = stepped(users_ref[...], total, noise_ref[...])

    [users_1] = call(
        user_step,
        [(users.shape, f32)],
        [place, local(users_0), local(items_0), local(noise_users_0)]
        + [local(v) for v in errors_0 + errors_1 + errors_2 + errors_3],
        SHORT * unit,
        after=moved,
    )
    users_s = swap(users_1, 1)

    moved += move(1, [users_1])
    ahead = [onward(value) for value in moved]

    def late(k, slot, place_ref, items_ref, users_ref, users_s_ref, rating_ref, weight_ref,
             rating_s_ref, weight_s_ref, *rest):
        high_out, low_out, copy_out, out = rest[-4:]
        own, other = halves(users_ref[...]), halves(users_s_ref[...])
        now = items_ref[...]
        copy_out[...] = now
        item_halves = halves(now)
        at = pl.ds(pl.multiple_of((place_ref[0] ^ (2 * slot)) * quarter + k * chunk, chunk), chunk)
        errors = errors_of(item_halves, own, rating_ref[at, :], weight_ref[at, :])
        high_out[...], low_out[...] = errors
        total = product(errors, own, NN)
        at = slice(slot * quarter + k * chunk, slot * quarter + (k + 1) * chunk)
        errors = errors_of(item_halves, other, rating_s_ref[at, :], weight_s_ref[at, :])
        total = total + product(errors, other, NN)
        if slot == 1:
            total = stepped(now, total, rest[0][k * chunk : (k + 1) * chunk, :])
        out[...] = total

    common = [local(v) for v in (users_1, users_s, rating_1, weight_1, rating_s, weight_s)]
    errors_shape = (chunk, owned)
    late_outs = [(errors_shape, bf16)] * 2 + [(piece, f32)] * 2
    def relay(value_ref, out):
        out[...] = value_ref[...]

    here, there = list(ahead), []
    errors_here, here_copy, sent = [], [], []
    for k in range(CHUNKS):
        if k:
            [here[k]] = call(relay, [(piece, f32)], [local(here[k])], 1, after=sent)
        there.append(swap(here[k], 2))
        high, low, rows, value = call(
            functools.partial(late, k, 0), late_outs, [place, local(here[k])] + common,
            4 * unit // CHUNKS, after=sent[-1:],
        )
        errors_here.append((high, low))
        here_copy.append(rows)
        sent.append(value)
    received = [swap(value, 2) for value in sent]
    errors_there, there_copy, finished = [], [], []
    for k in range(CHUNKS):
        high, low, rows, step = call(
            functools.partial(late, k, 1), late_outs,
            [place, local(there[k])] + common + [local(noise_1)], FAR[k] * unit,
            after=[sent[-1], *finished[-1:]],
        )
        [value] = call(add_scaled, [(piece, f32)], [local(step), local(received[k])], FIN * unit)
        errors_there.append((high, low))
        there_copy.append(rows)
        finished.append(value)
    final = [onward(value) for value in finished]
    here_s = [swap(value, 1) for value in here_copy]
    there_s = [swap(value, 1) for value in there_copy]

    def last(place_ref, rating_ref, weight_ref, users_ref, noise_hbm, *rest):
        known, blocks = rest[: 6 * CHUNKS], rest[6 * CHUNKS : 8 * CHUNKS]
        users_out, token, noise, sems = rest[8 * CHUNKS :]
        token[...] = jnp.zeros_like(token)
        [copy] = fetch([(noise_hbm.at[1], noise)], sems)
        user_halves = halves(users_ref[...])
        total = jnp.zeros((owned, rank), f32)
        for n in range(2 * CHUNKS):
            errors = (known[3 * n][...], known[3 * n + 1][...])
            total = total + product(errors, halves(known[3 * n + 2][...]), TN)
        for n, block in enumerate(blocks):
            flip, k = (1, 3)[n // CHUNKS], n % CHUNKS
            at = pl.ds(pl.multiple_of((place_ref[0] ^ flip) * quarter + k * chunk, chunk), chunk)
            item_halves = halves(block[...])
            errors = errors_of(item_halves, user_halves, rating_ref[at, :], weight_ref[at, :])
            total = total + product(errors, item_halves, TN)
        copy.wait()
        users_out[...] = stepped(users_ref[...], total, noise[...])

    known = [
        local(v)
        for errors, rows in zip(errors_here + errors_there, here + there)
        for v in (*errors, rows)
    ]
    users_out, token = call(
        last,
        [(users.shape, f32), ((8, 128), f32)],
        [place, local(rating_1), local(weight_1), local(users_1), (DISTANT, noise_users)]
        + known + [local(v) for v in here_s + there_s],
        LAST * unit,
        [pltpu.VMEM(users.shape, f32), pltpu.SemaphoreType.DMA((1,))],
        after=finished,
    )

    def gather(*refs):
        for k in range(CHUNKS):
            refs[-1][k * chunk : (k + 1) * chunk, :] = refs[k][...]

    [items_out] = call(
        gather, [((quarter, rank), f32)], [local(v) for v in final], 1, after=[token]
    )
    return (users_out, items_out)


def solution(mesh):
    in_specs = (
        P(("blk", "grp"), None),
        P("blk", None),
        P(None, ("blk", "grp"), None),
        P(None, "blk", None),
        P(None, ("blk", "grp")),
        P(None, ("blk", "grp")),
        P(None, ("blk", "grp"), None, None),
        P(None, ("blk", "grp"), None, None),
    )
    out_specs = (P(("blk", "grp"), None), P(("blk", "grp"), None))
    return jax.shard_map(body, mesh=mesh, in_specs=in_specs, out_specs=out_specs, check_vma=False)
```

```python
import functools
import math

import jax
import jax.numpy as jnp
from jax import lax
from jax.experimental import pallas as pl
from jax.experimental.pallas import tpu as pltpu
from jax.sharding import PartitionSpec as P

STEP_SIZE = 0.001
LIKELIHOOD = 20.0
NOISE_SCALE = math.sqrt(0.002)
GAIN = STEP_SIZE * LIKELIHOOD
AXES = ("blk", "grp")
TILE = 128
CHUNKS = 2
WEIGHT = 8
COST = {"part": 2, "join": 0, "join_2": 16, "part_2": 2, "move": (4, 4, 4, 4), "user_step": 0, "layout": 0, "near": (2, 2), "far": (2, 2), "finish": 0, "last": 0, "final": 0}
VMEM_LIMIT = 16 * 1024 * 1024

NN = (((1,), (0,)), ((), ()))
NT = (((1,), (1,)), ((), ()))
TN = (((0,), (0,)), ((), ()))


def halves(value):
    high = value.astype(jnp.bfloat16)
    low = (value - high.astype(jnp.float32)).astype(jnp.bfloat16)
    return high, low


def product(left, right, dims):
    dot = functools.partial(
        lax.dot_general, dimension_numbers=dims, preferred_element_type=jnp.float32
    )
    return dot(left[0], right[0]) + (dot(left[0], right[1]) + dot(left[1], right[0]))


def errors_of(item_halves, user_halves, rating, weight):
    predicted = product(item_halves, user_halves, NT)
    return halves(weight.astype(jnp.float32) * (rating.astype(jnp.float32) - predicted))


def stepped(now, total, noise):
    return now + STEP_SIZE * (LIKELIHOOD * total - now) + NOISE_SCALE * noise


SCALARS = pl.BlockSpec(memory_space=pltpu.SMEM)
LOCAL = pl.BlockSpec(memory_space=pltpu.VMEM)
DISTANT = pl.BlockSpec(memory_space=pltpu.HBM)
AFTER = pl.BlockSpec(memory_space=pl.ANY)


def call(body, outs, operands, cost, scratch=(), after=()):
    unread = len(after)

    def kernel(*refs):
        body(*refs[unread:])

    return pl.pallas_call(
        kernel,
        in_specs=[AFTER] * unread + [spec for spec, _ in operands],
        out_specs=[LOCAL] * len(outs),
        out_shape=[jax.ShapeDtypeStruct(shape, dtype) for shape, dtype in outs],
        scratch_shapes=list(scratch),
        compiler_params=pltpu.CompilerParams(vmem_limit_bytes=VMEM_LIMIT),
        cost_estimate=pl.CostEstimate(
            flops=WEIGHT * cost, bytes_accessed=1 << 18, transcendentals=0
        ),
        name=body.__name__ if hasattr(body, "__name__") else body.func.__name__,
    )(*after, *[held(spec, array) for spec, array in operands])


def held(spec, array):
    return pltpu.with_memory_space_constraint(array, pltpu.HBM) if spec is DISTANT else array


def local(array):
    return (LOCAL, array)


def body(users, items, noise_users, noise_items, tile_index, counts, ratings, weights):
    f32, bf16 = jnp.float32, jnp.bfloat16
    n_blk, n_grp = lax.axis_size("blk"), lax.axis_size("grp")
    owned, rank = users.shape
    slots = ratings.shape[1]
    columns = items.shape[0] // TILE
    per_quarter = columns // n_grp
    quarter = per_quarter * TILE
    chunk = quarter // CHUNKS
    place = (SCALARS, lax.axis_index("grp").astype(jnp.int32).reshape(1))

    def swap(value, other):
        pairs = [
            (b * n_grp + g, b * n_grp + (g ^ other)) for b in range(n_blk) for g in range(n_grp)
        ]
        with jax.named_scope("core_swap" if other == 1 else "chip_swap"):
            return lax.ppermute(value, AXES, pairs)

    def onward(value):
        pairs = [
            (b * n_grp + g, (b + 1) % n_blk * n_grp + (g ^ 2))
            for b in range(n_blk)
            for g in range(n_grp)
        ]
        with jax.named_scope("onward"):
            return lax.ppermute(value, AXES, pairs)

    dense = (columns, owned, TILE)
    piece = (chunk, rank)
    square = (quarter, owned)
    unit = 2 * owned * quarter * rank * 3

    def rows_of(place_ref, flip):
        return pl.ds(pl.multiple_of((place_ref[0] ^ flip) * quarter, quarter), quarter)

    def side_by_side(dense_ref, start):
        return jnp.concatenate([dense_ref[start + t] for t in range(per_quarter)], 1)

    def quarter_terms(place_ref, flip, rating_ref, weight_ref, users_ref, items_ref, high_ref, low_ref):
        start = (place_ref[0] ^ flip) * per_quarter
        user_halves = halves(users_ref[...])
        item_halves = halves(items_ref[rows_of(place_ref, flip), :])
        rating = side_by_side(rating_ref, start).astype(f32).T
        weight = side_by_side(weight_ref, start).astype(f32).T
        errors = errors_of(item_halves, user_halves, rating, weight)
        high_ref[...], low_ref[...] = errors
        return product(errors, user_halves, NN)

    def fetch(pairs, sems):
        copies = [pltpu.make_async_copy(a, b, sems.at[n]) for n, (a, b) in enumerate(pairs)]
        for copy in copies:
            copy.start()
        return copies

    live = counts.reshape(-1)
    tables = [(DISTANT, tile_index), (DISTANT, live), (DISTANT, ratings), (DISTANT, weights)]
    landing = [
        pltpu.SMEM(tile_index.shape, jnp.int32),
        pltpu.SMEM(live.shape, jnp.int32),
        pltpu.VMEM(ratings.shape[1:], bf16),
        pltpu.VMEM(weights.shape[1:], bf16),
    ]

    def first(place_ref, index_hbm, count_hbm, rating_hbm, weight_hbm, users_hbm, items_hbm, noise_hbm,
              rating_out, weight_out, users_out, items_out, noise_out, high_out, low_out, grads_out,
              index_ref, count_ref, rating_in, weight_in, sems):
        copies = fetch(
            [(index_hbm, index_ref), (count_hbm, count_ref),
             (rating_hbm.at[0], rating_in), (weight_hbm.at[0], weight_in),
             (users_hbm, users_out), (items_hbm, items_out),
             (noise_hbm.at[0, rows_of(place_ref, 2), :], noise_out.at[:quarter, :]),
             (noise_hbm.at[0, rows_of(place_ref, 0), :], noise_out.at[quarter:, :])],
            sems,
        )
        rating_out[...] = jnp.zeros_like(rating_out)
        weight_out[...] = jnp.zeros_like(weight_out)
        for copy in copies[:4]:
            copy.wait()
        for slot in range(slots):

            @pl.when(slot < count_ref[0])
            def _(slot=slot):
                tile = index_ref[0, slot]
                column = lax.rem(tile, columns)
                row = pl.multiple_of(lax.div(tile, columns) * TILE, TILE)
                rating_out[column, pl.ds(row, TILE), :] = rating_in[slot]
                weight_out[column, pl.ds(row, TILE), :] = weight_in[slot]

        copies[4].wait()
        copies[5].wait()
        grads_out[...] = quarter_terms(
            place_ref, 1, rating_out, weight_out, users_out, items_out, high_out, low_out
        )
        copies[6].wait()
        copies[7].wait()

    part_outs = [(square, bf16)] * 2 + [((quarter, rank), f32)]
    rating_0, weight_0, users_0, items_0, noise_0, *errors_1, to_sibling = call(
        first,
        [(dense, bf16)] * 2 + [(users.shape, f32), (items.shape, f32), ((2 * quarter, rank), f32)] + part_outs,
        [place] + tables + [(DISTANT, v) for v in (users, items, noise_items)],
        2 * unit,
        landing + [pltpu.SemaphoreType.DMA((8,))],
    )
    from_sibling_0 = swap(to_sibling, 1)
    stage_0 = [local(rating_0), local(weight_0), local(users_0), local(items_0)]

    def part(flip, place_ref, *refs):
        refs[-1][...] = quarter_terms(place_ref, flip, *refs[:-1])

    def quarter_part(flip, cost, after):
        high, low, grads = call(
            functools.partial(part, flip), part_outs, [place] + stage_0, cost * unit, after=after
        )
        return [high, low], grads

    def join(at, a_ref, b_ref, out):
        out[...] = a_ref[at, :] + b_ref[at, :]

    def add_scaled(at, base_ref, a_ref, out):
        out[...] = base_ref[at, :] + GAIN * a_ref[at, :]

    def rows(k):
        return slice(k * chunk, (k + 1) * chunk)

    def joined(kernel, at, a, b, cost, after):
        return call(
            functools.partial(kernel, at), [(piece, f32)], [local(a), local(b)], cost * unit,
            after=after,
        )

    errors_3, to_sibling = quarter_part(3, COST["part"], [])
    from_sibling_2 = swap(to_sibling, 1)
    errors_0, mine = quarter_part(0, COST["part"], [to_sibling])
    to_chip = []
    for k in range(CHUNKS):
        to_chip += joined(join, rows(k), mine, from_sibling_0, COST["join"], to_chip[-1:])
    from_chip = [swap(value, 2) for value in to_chip]
    errors_2, mine = quarter_part(2, COST["part_2"], to_chip)

    def user_step(place_ref, users_ref, items_ref, noise_ref, *rest):
        errors, users_out = rest[:-1], rest[-1]
        total = jnp.zeros((owned, rank), f32)
        for flip in range(n_grp):
            item_halves = halves(items_ref[rows_of(place_ref, flip), :])
            kept = (errors[2 * flip][...], errors[2 * flip + 1][...])
            total = total + product(kept, item_halves, TN)
        users_out[...] = stepped(users_ref[...], total, noise_ref[...])

    [users_1] = call(
        user_step,
        [(users.shape, f32)],
        [place, local(users_0), local(items_0), local(noise_users[0])]
        + [local(v) for v in errors_0 + errors_1 + errors_2 + errors_3],
        COST["user_step"] * unit,
    )
    flat = (columns * TILE, owned)

    def layout(place_ref, index_hbm, count_hbm, noise_hbm, rating_ref, weight_ref, users_ref,
               rating_out, weight_out, send_out, noise_out, index_ref, count_ref, sems):
        copies = fetch(
            [(index_hbm, index_ref), (count_hbm, count_ref),
             (noise_hbm.at[1, rows_of(place_ref, 2), :], noise_out)],
            sems,
        )
        rating_out[...] = jnp.zeros_like(rating_out)
        weight_out[...] = jnp.zeros_like(weight_out)
        for copy in copies[:2]:
            copy.wait()
        for slot in range(slots):

            @pl.when(slot < count_ref[1])
            def _(slot=slot):
                tile = index_ref[1, slot]
                at = pl.ds(pl.multiple_of(lax.rem(tile, columns) * TILE, TILE), TILE)
                turned = (rating_ref[slot].astype(f32).T, weight_ref[slot].astype(f32).T)
                for row in range(owned // TILE):

                    @pl.when(lax.div(tile, columns) == row)
                    def _(row=row):
                        across = slice(row * TILE, (row + 1) * TILE)
                        rating_out[at, across] = turned[0]
                        weight_out[at, across] = turned[1]

        for n, flip in enumerate((1, 3)):
            for offset, values in ((0, rating_out), (2 * quarter, weight_out)):
                at = slice(offset + n * quarter, offset + (n + 1) * quarter)
                send_out[at, :] = values[rows_of(place_ref, flip), :]
        send_out[4 * quarter :, :] = users_ref[...]
        copies[2].wait()

    rating_1, weight_1, to_sibling, noise_1 = call(
        layout,
        [(flat, f32)] * 2 + [((4 * quarter + owned, rank), f32), ((quarter, rank), f32)],
        [place] + tables[:2] + [(DISTANT, noise_items)]
        + [local(v) for v in (ratings[1], weights[1], users_1)],
        COST["layout"] * unit,
        landing[:2] + [pltpu.SemaphoreType.DMA((3,))],
        after=[users_1],
    )
    from_sibling = swap(to_sibling, 1)

    def move(n, place_ref, items_ref, noise_ref, own_ref, other_ref, out):
        flip, k = (2, 0)[n // CHUNKS], n % CHUNKS
        start = pl.multiple_of((place_ref[0] ^ flip) * quarter + k * chunk, chunk)
        total = own_ref[...] + other_ref[...]
        out[...] = stepped(items_ref[pl.ds(start, chunk), :], total, noise_ref[rows(n), :])

    moved = []
    for n in range(2 * CHUNKS):
        if n < CHUNKS:
            to_chip += joined(
                join, rows(n), mine, from_sibling_2, COST["join_2"],
                [to_sibling, from_chip[n], *moved[-1:]],
            )
            from_chip.append(swap(to_chip[-1], 2))
        terms = [local(v) for v in (items_0, noise_0, to_chip[(n + CHUNKS) % (2 * CHUNKS)], from_chip[n])]
        moved += call(
            functools.partial(move, n), [(piece, f32)], [place] + terms, COST["move"][n] * unit,
            after=moved[-1:],
        )
    ahead = [onward(value) for value in moved]

    def late(k, slot, place_ref, items_ref, users_ref, rating_ref, weight_ref, sibling_ref, *rest):
        high_out, low_out, out = rest[-3:]
        own, other = halves(users_ref[...]), halves(sibling_ref[4 * quarter :, :])
        now = items_ref[...]
        item_halves = halves(now)
        at = pl.ds(pl.multiple_of((place_ref[0] ^ (2 * slot)) * quarter + k * chunk, chunk), chunk)
        errors = errors_of(item_halves, own, rating_ref[at, :], weight_ref[at, :])
        high_out[...], low_out[...] = errors
        total = product(errors, own, NN)
        at = slot * quarter + k * chunk
        rating = sibling_ref[at : at + chunk, :]
        weight = sibling_ref[2 * quarter + at : 2 * quarter + at + chunk, :]
        errors = errors_of(item_halves, other, rating, weight)
        total = total + product(errors, other, NN)
        if slot == 1:
            total = stepped(now, total, rest[0][rows(k), :])
        out[...] = total

    common = [local(v) for v in (users_1, rating_1, weight_1, from_sibling)]
    errors_shape = (chunk, owned)
    late_outs = [(errors_shape, bf16)] * 2 + [(piece, f32)]
    def relay(value_ref, out):
        out[...] = value_ref[...]

    def relayed(value, cost, after):
        return call(relay, [(piece, f32)], [local(value)], cost * unit, after=after)

    here, there = ahead[:CHUNKS], ahead[CHUNKS:]
    errors_here, sent = [], []
    for k in range(CHUNKS):
        high, low, value = call(
            functools.partial(late, k, 0), late_outs, [place, local(here[k])] + common,
            COST["near"][k] * unit, after=sent[-1:],
        )
        errors_here.append((high, low))
        sent.append(value)
    received = [swap(value, 2) for value in sent]
    errors_there, finished = [], []
    for k in range(CHUNKS):
        high, low, value = call(
            functools.partial(late, k, 1), late_outs,
            [place, local(there[k])] + common + [local(noise_1)], COST["far"][k] * unit,
            after=[sent[-1], *finished[-1:]],
        )
        errors_there.append((high, low))
        finished += joined(add_scaled, rows(0), value, received[k], COST["finish"], [])
    final = [onward(value) for value in finished]

    def stack(*refs):
        for k in range(CHUNKS):
            refs[-1][rows(k), :] = refs[k][...]

    def paired(values, after):
        [value] = call(stack, [((quarter, rank), f32)], [local(v) for v in values], 1, after=after)
        return swap(value, 1)

    here_s, there_s = paired(here, sent[-1:]), paired(there, finished[:1])

    def last(place_ref, rating_ref, weight_ref, users_ref, noise_hbm, *rest):
        known, blocks = rest[: 6 * CHUNKS], rest[6 * CHUNKS : 6 * CHUNKS + 2]
        users_out, token, noise, sems = rest[6 * CHUNKS + 2 :]
        token[...] = jnp.zeros_like(token)
        [copy] = fetch([(noise_hbm.at[1], noise)], sems)
        user_halves = halves(users_ref[...])
        total = jnp.zeros((owned, rank), f32)
        for n in range(2 * CHUNKS):
            errors = (known[3 * n][...], known[3 * n + 1][...])
            total = total + product(errors, halves(known[3 * n + 2][...]), TN)
        for block, flip in zip(blocks, (1, 3)):
            at = rows_of(place_ref, flip)
            item_halves = halves(block[...])
            errors = errors_of(item_halves, user_halves, rating_ref[at, :], weight_ref[at, :])
            total = total + product(errors, item_halves, TN)
        copy.wait()
        users_out[...] = stepped(users_ref[...], total, noise[...])

    known = [
        local(v)
        for errors, values in zip(errors_here + errors_there, here + there)
        for v in (*errors, values)
    ]
    users_out, token = call(
        last,
        [(users.shape, f32), ((8, 128), f32)],
        [place, local(rating_1), local(weight_1), local(users_1), (DISTANT, noise_users)]
        + known + [local(here_s), local(there_s)],
        COST["last"] * unit,
        [pltpu.VMEM(users.shape, f32), pltpu.SemaphoreType.DMA((1,))],
        after=finished,
    )

    [early] = relayed(final[0], COST["final"], [token])
    [items_out] = call(stack, [((quarter, rank), f32)], [local(early), local(final[1])], 1)
    return (users_out, items_out)


def solution(mesh):
    in_specs = (
        P(("blk", "grp"), None),
        P("blk", None),
        P(None, ("blk", "grp"), None),
        P(None, "blk", None),
        P(None, ("blk", "grp")),
        P(None, ("blk", "grp")),
        P(None, ("blk", "grp"), None, None),
        P(None, ("blk", "grp"), None, None),
    )
    out_specs = (P(("blk", "grp"), None), P(("blk", "grp"), None))
    return jax.shard_map(body, mesh=mesh, in_specs=in_specs, out_specs=out_specs, check_vma=False)
```

```python
import functools
import math

import jax
import jax.numpy as jnp
from jax import lax
from jax.experimental import pallas as pl
from jax.experimental.pallas import tpu as pltpu
from jax.sharding import PartitionSpec as P

STEP_SIZE = 0.001
LIKELIHOOD = 20.0
NOISE_SCALE = math.sqrt(0.002)
GAIN = STEP_SIZE * LIKELIHOOD
AXES = ("blk", "grp")
TILE = 128
CHUNKS = 2
SHARES = 3
WEIGHT = 8
COST = {"part": 2, "join": 0, "join_2": 16, "part_2": 2, "move": (4, 4, 4, 4), "user_step": 0, "layout": 0, "near": (2, 2), "far": (2, 2), "finish": 0, "user_sums": 64, "last": 0, "final": 0}
VMEM_LIMIT = 16 * 1024 * 1024

NN = (((1,), (0,)), ((), ()))
NT = (((1,), (1,)), ((), ()))
TN = (((0,), (0,)), ((), ()))


def halves(value):
    high = value.astype(jnp.bfloat16)
    low = (value - high.astype(jnp.float32)).astype(jnp.bfloat16)
    return high, low


def product(left, right, dims):
    dot = functools.partial(
        lax.dot_general, dimension_numbers=dims, preferred_element_type=jnp.float32
    )
    return dot(left[0], right[0]) + (dot(left[0], right[1]) + dot(left[1], right[0]))


def errors_of(item_halves, user_halves, rating, weight):
    predicted = product(item_halves, user_halves, NT)
    return halves(weight.astype(jnp.float32) * (rating.astype(jnp.float32) - predicted))


def stepped(now, total, noise):
    return now + STEP_SIZE * (LIKELIHOOD * total - now) + NOISE_SCALE * noise


SCALARS = pl.BlockSpec(memory_space=pltpu.SMEM)
LOCAL = pl.BlockSpec(memory_space=pltpu.VMEM)
DISTANT = pl.BlockSpec(memory_space=pltpu.HBM)
AFTER = pl.BlockSpec(memory_space=pl.ANY)


def call(body, outs, operands, cost, scratch=(), after=()):
    unread = len(after)

    def kernel(*refs):
        body(*refs[unread:])

    return pl.pallas_call(
        kernel,
        in_specs=[AFTER] * unread + [spec for spec, _ in operands],
        out_specs=[LOCAL] * len(outs),
        out_shape=[jax.ShapeDtypeStruct(shape, dtype) for shape, dtype in outs],
        scratch_shapes=list(scratch),
        compiler_params=pltpu.CompilerParams(vmem_limit_bytes=VMEM_LIMIT),
        cost_estimate=pl.CostEstimate(
            flops=WEIGHT * cost, bytes_accessed=1 << 18, transcendentals=0
        ),
        name=body.__name__ if hasattr(body, "__name__") else body.func.__name__,
    )(*after, *[held(spec, array) for spec, array in operands])


def held(spec, array):
    return pltpu.with_memory_space_constraint(array, pltpu.HBM) if spec is DISTANT else array


def local(array):
    return (LOCAL, array)


def body(users, items, noise_users, noise_items, tile_index, counts, ratings, weights):
    f32, bf16 = jnp.float32, jnp.bfloat16
    n_blk, n_grp = lax.axis_size("blk"), lax.axis_size("grp")
    owned, rank = users.shape
    slots = ratings.shape[1]
    columns = items.shape[0] // TILE
    per_quarter = columns // n_grp
    quarter = per_quarter * TILE
    chunk = quarter // CHUNKS
    place = (SCALARS, lax.axis_index("grp").astype(jnp.int32).reshape(1))

    def swap(value, other):
        pairs = [
            (b * n_grp + g, b * n_grp + (g ^ other)) for b in range(n_blk) for g in range(n_grp)
        ]
        with jax.named_scope("core_swap" if other == 1 else "chip_swap"):
            return lax.ppermute(value, AXES, pairs)

    def onward(value):
        pairs = [
            (b * n_grp + g, (b + 1) % n_blk * n_grp + (g ^ 2))
            for b in range(n_blk)
            for g in range(n_grp)
        ]
        with jax.named_scope("onward"):
            return lax.ppermute(value, AXES, pairs)

    dense = (columns, owned, TILE)
    piece = (chunk, rank)
    square = (quarter, owned)
    unit = 2 * owned * quarter * rank * 3

    def rows_of(place_ref, flip):
        return pl.ds(pl.multiple_of((place_ref[0] ^ flip) * quarter, quarter), quarter)

    def side_by_side(dense_ref, start):
        return jnp.concatenate([dense_ref[start + t] for t in range(per_quarter)], 1)

    def quarter_terms(place_ref, flip, rating_ref, weight_ref, users_ref, items_ref, high_ref, low_ref):
        start = (place_ref[0] ^ flip) * per_quarter
        user_halves = halves(users_ref[...])
        item_halves = halves(items_ref[rows_of(place_ref, flip), :])
        rating = side_by_side(rating_ref, start).astype(f32).T
        weight = side_by_side(weight_ref, start).astype(f32).T
        errors = errors_of(item_halves, user_halves, rating, weight)
        high_ref[...], low_ref[...] = errors
        return product(errors, user_halves, NN)

    def fetch(pairs, sems):
        copies = [pltpu.make_async_copy(a, b, sems.at[n]) for n, (a, b) in enumerate(pairs)]
        for copy in copies:
            copy.start()
        return copies

    live = counts.reshape(-1)
    tables = [(DISTANT, tile_index), (DISTANT, live), (DISTANT, ratings), (DISTANT, weights)]
    landing = [
        pltpu.SMEM(tile_index.shape, jnp.int32),
        pltpu.SMEM(live.shape, jnp.int32),
        pltpu.VMEM(ratings.shape[1:], bf16),
        pltpu.VMEM(weights.shape[1:], bf16),
    ]

    def first(place_ref, index_hbm, count_hbm, rating_hbm, weight_hbm, users_hbm, items_hbm, noise_hbm,
              rating_out, weight_out, users_out, items_out, noise_out, high_out, low_out, grads_out,
              index_ref, count_ref, rating_in, weight_in, sems):
        copies = fetch(
            [(index_hbm, index_ref), (count_hbm, count_ref),
             (rating_hbm.at[0], rating_in), (weight_hbm.at[0], weight_in), (users_hbm, users_out)]
            + [(items_hbm.at[rows_of(place_ref, flip), :], items_out.at[rows_of(place_ref, flip), :])
               for flip in (1, 0, 3, 2)]
            + [(noise_hbm.at[0, rows_of(place_ref, 2), :], noise_out.at[:quarter, :]),
               (noise_hbm.at[0, rows_of(place_ref, 0), :], noise_out.at[quarter:, :])],
            sems,
        )
        rating_out[...] = jnp.zeros_like(rating_out)
        weight_out[...] = jnp.zeros_like(weight_out)
        for copy in copies[:4]:
            copy.wait()
        for slot in range(slots):

            @pl.when(slot < count_ref[0])
            def _(slot=slot):
                tile = index_ref[0, slot]
                column = lax.rem(tile, columns)
                row = pl.multiple_of(lax.div(tile, columns) * TILE, TILE)
                rating_out[column, pl.ds(row, TILE), :] = rating_in[slot]
                weight_out[column, pl.ds(row, TILE), :] = weight_in[slot]

        copies[4].wait()
        copies[5].wait()
        grads_out[...] = quarter_terms(
            place_ref, 1, rating_out, weight_out, users_out, items_out, high_out, low_out
        )
        for copy in copies[6:]:
            copy.wait()

    part_outs = [(square, bf16)] * 2 + [((quarter, rank), f32)]
    rating_0, weight_0, users_0, items_0, noise_0, *errors_1, to_sibling = call(
        first,
        [(dense, bf16)] * 2 + [(users.shape, f32), (items.shape, f32), ((2 * quarter, rank), f32)] + part_outs,
        [place] + tables + [(DISTANT, v) for v in (users, items, noise_items)],
        2 * unit,
        landing + [pltpu.SemaphoreType.DMA((11,))],
    )
    from_sibling_0 = swap(to_sibling, 1)
    stage_0 = [local(rating_0), local(weight_0), local(users_0), local(items_0)]

    def part(flip, place_ref, *refs):
        refs[-1][...] = quarter_terms(place_ref, flip, *refs[:-1])

    def quarter_part(flip, cost, after):
        high, low, grads = call(
            functools.partial(part, flip), part_outs, [place] + stage_0, cost * unit, after=after
        )
        return [high, low], grads

    def join(at, a_ref, b_ref, out):
        out[...] = a_ref[at, :] + b_ref[at, :]

    def add_scaled(at, base_ref, a_ref, out):
        out[...] = base_ref[at, :] + GAIN * a_ref[at, :]

    def rows(k):
        return slice(k * chunk, (k + 1) * chunk)

    def joined(kernel, at, a, b, cost, after):
        return call(
            functools.partial(kernel, at), [(piece, f32)], [local(a), local(b)], cost * unit,
            after=after,
        )

    errors_3, to_sibling = quarter_part(3, COST["part"], [])
    from_sibling_2 = swap(to_sibling, 1)
    errors_0, mine = quarter_part(0, COST["part"], [to_sibling])
    to_chip = []
    for k in range(CHUNKS):
        to_chip += joined(join, rows(k), mine, from_sibling_0, COST["join"], to_chip[-1:])
    from_chip = [swap(value, 2) for value in to_chip]
    errors_2, mine = quarter_part(2, COST["part_2"], to_chip)

    def user_step(place_ref, users_ref, items_ref, noise_ref, *rest):
        errors, users_out = rest[:-1], rest[-1]
        total = jnp.zeros((owned, rank), f32)
        for flip in range(n_grp):
            item_halves = halves(items_ref[rows_of(place_ref, flip), :])
            kept = (errors[2 * flip][...], errors[2 * flip + 1][...])
            total = total + product(kept, item_halves, TN)
        users_out[...] = stepped(users_ref[...], total, noise_ref[...])

    [users_1] = call(
        user_step,
        [(users.shape, f32)],
        [place, local(users_0), local(items_0), local(noise_users[0])]
        + [local(v) for v in errors_0 + errors_1 + errors_2 + errors_3],
        COST["user_step"] * unit,
    )
    flat = (columns * TILE, owned)

    def layout(place_ref, index_hbm, count_hbm, noise_hbm, rating_ref, weight_ref, users_ref,
               rating_out, weight_out, send_out, noise_out, index_ref, count_ref, sems):
        copies = fetch(
            [(index_hbm, index_ref), (count_hbm, count_ref),
             (noise_hbm.at[1, rows_of(place_ref, 2), :], noise_out)],
            sems,
        )
        rating_out[...] = jnp.zeros_like(rating_out)
        weight_out[...] = jnp.zeros_like(weight_out)
        for copy in copies[:2]:
            copy.wait()
        for slot in range(slots):

            @pl.when(slot < count_ref[1])
            def _(slot=slot):
                tile = index_ref[1, slot]
                at = pl.ds(pl.multiple_of(lax.rem(tile, columns) * TILE, TILE), TILE)
                turned = (rating_ref[slot].astype(f32).T, weight_ref[slot].astype(f32).T)
                for row in range(owned // TILE):

                    @pl.when(lax.div(tile, columns) == row)
                    def _(row=row):
                        across = slice(row * TILE, (row + 1) * TILE)
                        rating_out[at, across] = turned[0]
                        weight_out[at, across] = turned[1]

        for n, flip in enumerate((1, 3)):
            for offset, values in ((0, rating_out), (2 * quarter, weight_out)):
                at = slice(offset + n * quarter, offset + (n + 1) * quarter)
                send_out[at, :] = values[rows_of(place_ref, flip), :]
        send_out[4 * quarter :, :] = users_ref[...]
        copies[2].wait()

    rating_1, weight_1, to_sibling, noise_1 = call(
        layout,
        [(flat, f32)] * 2 + [((4 * quarter + owned, rank), f32), ((quarter, rank), f32)],
        [place] + tables[:2] + [(DISTANT, noise_items)]
        + [local(v) for v in (ratings[1], weights[1], users_1)],
        COST["layout"] * unit,
        landing[:2] + [pltpu.SemaphoreType.DMA((3,))],
        after=[users_1],
    )
    from_sibling = swap(to_sibling, 1)

    def move(n, place_ref, items_ref, noise_ref, own_ref, other_ref, out):
        flip, k = (2, 0)[n // CHUNKS], n % CHUNKS
        start = pl.multiple_of((place_ref[0] ^ flip) * quarter + k * chunk, chunk)
        total = own_ref[...] + other_ref[...]
        out[...] = stepped(items_ref[pl.ds(start, chunk), :], total, noise_ref[rows(n), :])

    moved = []
    for n in range(2 * CHUNKS):
        if n < CHUNKS:
            to_chip += joined(
                join, rows(n), mine, from_sibling_2, COST["join_2"],
                [to_sibling, from_chip[n], *moved[-1:]],
            )
            from_chip.append(swap(to_chip[-1], 2))
        terms = [local(v) for v in (items_0, noise_0, to_chip[(n + CHUNKS) % (2 * CHUNKS)], from_chip[n])]
        moved += call(
            functools.partial(move, n), [(piece, f32)], [place] + terms, COST["move"][n] * unit,
            after=moved[-1:],
        )
    ahead = [onward(value) for value in moved]

    def late(k, slot, place_ref, items_ref, users_ref, rating_ref, weight_ref, sibling_ref, *rest):
        high_out, low_out, high_s_out, low_s_out, out = rest[-5:]
        own, other = halves(users_ref[...]), halves(sibling_ref[4 * quarter :, :])
        now = items_ref[...]
        item_halves = halves(now)
        at = pl.ds(pl.multiple_of((place_ref[0] ^ (2 * slot)) * quarter + k * chunk, chunk), chunk)
        errors = errors_of(item_halves, own, rating_ref[at, :], weight_ref[at, :])
        high_out[...], low_out[...] = errors
        total = product(errors, own, NN)
        at = slot * quarter + k * chunk
        rating = sibling_ref[at : at + chunk, :]
        weight = sibling_ref[2 * quarter + at : 2 * quarter + at + chunk, :]
        errors = errors_of(item_halves, other, rating, weight)
        high_s_out[...], low_s_out[...] = errors
        total = total + product(errors, other, NN)
        if slot == 1:
            total = stepped(now, total, rest[0][rows(k), :])
        out[...] = total

    common = [local(v) for v in (users_1, rating_1, weight_1, from_sibling)]
    errors_shape = (chunk, owned)
    late_outs = [(errors_shape, bf16)] * 4 + [(piece, f32)]
    def relay(value_ref, out):
        out[...] = value_ref[...]

    def relayed(value, cost, after):
        return call(relay, [(piece, f32)], [local(value)], cost * unit, after=after)

    here, there = ahead[:CHUNKS], ahead[CHUNKS:]
    errors_here, sent = [], []
    for k in range(CHUNKS):
        *errors, value = call(
            functools.partial(late, k, 0), late_outs, [place, local(here[k])] + common,
            COST["near"][k] * unit, after=sent[-1:],
        )
        errors_here.append(errors)
        sent.append(value)
    received = [swap(value, 2) for value in sent]
    errors_there, finished = [], []
    for k in range(CHUNKS):
        *errors, value = call(
            functools.partial(late, k, 1), late_outs,
            [place, local(there[k])] + common + [local(noise_1)], COST["far"][k] * unit,
            after=[sent[-1], *finished[-1:]],
        )
        errors_there.append(errors)
        finished += joined(add_scaled, rows(0), value, received[k], COST["finish"], [])
    final = [onward(value) for value in finished]

    def stack(*refs):
        for k in range(CHUNKS):
            refs[-1][rows(k), :] = refs[k][...]

    known = [
        local(v)
        for errors, values in zip(errors_here + errors_there, here + there)
        for v in (*errors, values)
    ]
    step = -(-owned // (8 * SHARES)) * 8
    shares_at = [slice(n * step, min((n + 1) * step, owned)) for n in range(SHARES)]

    def user_sums(*refs):
        own = other = jnp.zeros((owned, rank), f32)
        for n in range(2 * CHUNKS):
            high, low, high_s, low_s, values = (ref[...] for ref in refs[5 * n : 5 * n + 5])
            item_halves = halves(values)
            own = own + product((high, low), item_halves, TN)
            other = other + product((high_s, low_s), item_halves, TN)
        refs[10 * CHUNKS][...] = own
        for n, ref in enumerate(refs[10 * CHUNKS + 1 :]):
            ref[...] = other[shares_at[n], :]

    sums, *to_sibling = call(
        user_sums, [(users.shape, f32)] + [((at.stop - at.start, rank), f32) for at in shares_at],
        known, COST["user_sums"] * unit,
        after=finished,
    )
    from_sibling = [swap(value, 1) for value in to_sibling]

    def last(users_ref, sums_ref, noise_ref, *rest):
        shares, (users_out, token) = rest[:SHARES], rest[SHARES:]
        token[...] = jnp.zeros_like(token)
        for at, ref in zip(shares_at, shares):
            total = sums_ref[at, :] + ref[...]
            users_out[at, :] = stepped(users_ref[at, :], total, noise_ref[at, :])

    users_out, token = call(
        last,
        [(users.shape, f32), ((8, 128), f32)],
        [local(users_1), local(sums), local(noise_users[1])] + [local(v) for v in from_sibling],
        COST["last"] * unit,
    )

    [early] = relayed(final[0], COST["final"], [token])
    [items_out] = call(stack, [((quarter, rank), f32)], [local(early), local(final[1])], 1)
    return (users_out, items_out)


def solution(mesh):
    in_specs = (
        P(("blk", "grp"), None),
        P("blk", None),
        P(None, ("blk", "grp"), None),
        P(None, "blk", None),
        P(None, ("blk", "grp")),
        P(None, ("blk", "grp")),
        P(None, ("blk", "grp"), None, None),
        P(None, ("blk", "grp"), None, None),
    )
    out_specs = (P(("blk", "grp"), None), P(("blk", "grp"), None))
    return jax.shard_map(body, mesh=mesh, in_specs=in_specs, out_specs=out_specs, check_vma=False)
```

```python
import functools
import math

import jax
import jax.numpy as jnp
from jax import lax
from jax.experimental import pallas as pl
from jax.experimental.pallas import tpu as pltpu
from jax.sharding import PartitionSpec as P

STEP_SIZE = 0.001
LIKELIHOOD = 20.0
NOISE_SCALE = math.sqrt(0.002)
GAIN = STEP_SIZE * LIKELIHOOD
AXES = ("blk", "grp")
TILE = 128
CHUNKS = 2
SHARES = 3
WEIGHT = 8
COST = {"part": 2, "join": 0, "join_2": 4, "relay": 1, "part_2": 2, "move": (4, 4, 4, 4), "user_step": 0, "layout": 0, "near": (2, 2), "far": (2, 2), "finish": 0, "user_sums": 64, "last": 0, "final": 0}
VMEM_LIMIT = 16 * 1024 * 1024

NN = (((1,), (0,)), ((), ()))
NT = (((1,), (1,)), ((), ()))
TN = (((0,), (0,)), ((), ()))


def halves(value):
    high = value.astype(jnp.bfloat16)
    low = (value - high.astype(jnp.float32)).astype(jnp.bfloat16)
    return high, low


def product(left, right, dims):
    dot = functools.partial(
        lax.dot_general, dimension_numbers=dims, preferred_element_type=jnp.float32
    )
    return dot(left[0], right[0]) + (dot(left[0], right[1]) + dot(left[1], right[0]))


def errors_of(item_halves, user_halves, rating, weight):
    predicted = product(item_halves, user_halves, NT)
    return halves(weight.astype(jnp.float32) * (rating.astype(jnp.float32) - predicted))


def stepped(now, total, noise):
    return now + STEP_SIZE * (LIKELIHOOD * total - now) + NOISE_SCALE * noise


SCALARS = pl.BlockSpec(memory_space=pltpu.SMEM)
LOCAL = pl.BlockSpec(memory_space=pltpu.VMEM)
DISTANT = pl.BlockSpec(memory_space=pltpu.HBM)
AFTER = pl.BlockSpec(memory_space=pl.ANY)


def call(body, outs, operands, cost, scratch=(), after=()):
    unread = len(after)

    def kernel(*refs):
        body(*refs[unread:])

    return pl.pallas_call(
        kernel,
        in_specs=[AFTER] * unread + [spec for spec, _ in operands],
        out_specs=[LOCAL] * len(outs),
        out_shape=[jax.ShapeDtypeStruct(shape, dtype) for shape, dtype in outs],
        scratch_shapes=list(scratch),
        compiler_params=pltpu.CompilerParams(vmem_limit_bytes=VMEM_LIMIT),
        cost_estimate=pl.CostEstimate(
            flops=WEIGHT * cost, bytes_accessed=1 << 18, transcendentals=0
        ),
        name=body.__name__ if hasattr(body, "__name__") else body.func.__name__,
    )(*after, *[held(spec, array) for spec, array in operands])


def held(spec, array):
    return pltpu.with_memory_space_constraint(array, pltpu.HBM) if spec is DISTANT else array


def local(array):
    return (LOCAL, array)


def body(users, items, noise_users, noise_items, tile_index, counts, ratings, weights):
    f32, bf16 = jnp.float32, jnp.bfloat16
    n_blk, n_grp = lax.axis_size("blk"), lax.axis_size("grp")
    owned, rank = users.shape
    slots = ratings.shape[1]
    columns = items.shape[0] // TILE
    per_quarter = columns // n_grp
    quarter = per_quarter * TILE
    chunk = quarter // CHUNKS
    place = (SCALARS, lax.axis_index("grp").astype(jnp.int32).reshape(1))

    def swap(value, other):
        pairs = [
            (b * n_grp + g, b * n_grp + (g ^ other)) for b in range(n_blk) for g in range(n_grp)
        ]
        with jax.named_scope("core_swap" if other == 1 else "chip_swap"):
            return lax.ppermute(value, AXES, pairs)

    def onward(value):
        pairs = [
            (b * n_grp + g, (b + 1) % n_blk * n_grp + (g ^ 2))
            for b in range(n_blk)
            for g in range(n_grp)
        ]
        with jax.named_scope("onward"):
            return lax.ppermute(value, AXES, pairs)

    dense = (columns, owned, TILE)
    piece = (chunk, rank)
    square = (quarter, owned)
    unit = 2 * owned * quarter * rank * 3

    def rows_of(place_ref, flip):
        return pl.ds(pl.multiple_of((place_ref[0] ^ flip) * quarter, quarter), quarter)

    def side_by_side(dense_ref, start):
        return jnp.concatenate([dense_ref[start + t] for t in range(per_quarter)], 1)

    def quarter_terms(place_ref, flip, rating_ref, weight_ref, users_ref, items_ref, high_ref, low_ref):
        start = (place_ref[0] ^ flip) * per_quarter
        user_halves = halves(users_ref[...])
        item_halves = halves(items_ref[rows_of(place_ref, flip), :])
        rating = side_by_side(rating_ref, start).astype(f32).T
        weight = side_by_side(weight_ref, start).astype(f32).T
        errors = errors_of(item_halves, user_halves, rating, weight)
        high_ref[...], low_ref[...] = errors
        return product(errors, user_halves, NN)

    def fetch(pairs, sems):
        copies = [pltpu.make_async_copy(a, b, sems.at[n]) for n, (a, b) in enumerate(pairs)]
        for copy in copies:
            copy.start()
        return copies

    live = counts.reshape(-1)
    tables = [(DISTANT, tile_index), (DISTANT, live), (DISTANT, ratings), (DISTANT, weights)]
    landing = [
        pltpu.SMEM(tile_index.shape, jnp.int32),
        pltpu.SMEM(live.shape, jnp.int32),
        pltpu.VMEM(ratings.shape[1:], bf16),
        pltpu.VMEM(weights.shape[1:], bf16),
    ]

    def first(place_ref, index_hbm, count_hbm, rating_hbm, weight_hbm, users_hbm, items_hbm, noise_hbm,
              rating_out, weight_out, users_out, items_out, noise_out, high_out, low_out, grads_out,
              index_ref, count_ref, rating_in, weight_in, sems):
        copies = fetch(
            [(index_hbm, index_ref), (count_hbm, count_ref),
             (rating_hbm.at[0], rating_in), (weight_hbm.at[0], weight_in), (users_hbm, users_out)]
            + [(items_hbm.at[rows_of(place_ref, flip), :], items_out.at[rows_of(place_ref, flip), :])
               for flip in (1, 0, 3, 2)]
            + [(noise_hbm.at[0, rows_of(place_ref, 2), :], noise_out.at[:quarter, :]),
               (noise_hbm.at[0, rows_of(place_ref, 0), :], noise_out.at[quarter:, :])],
            sems,
        )
        rating_out[...] = jnp.zeros_like(rating_out)
        weight_out[...] = jnp.zeros_like(weight_out)
        for copy in copies[:4]:
            copy.wait()
        for slot in range(slots):

            @pl.when(slot < count_ref[0])
            def _(slot=slot):
                tile = index_ref[0, slot]
                column = lax.rem(tile, columns)
                row = pl.multiple_of(lax.div(tile, columns) * TILE, TILE)
                rating_out[column, pl.ds(row, TILE), :] = rating_in[slot]
                weight_out[column, pl.ds(row, TILE), :] = weight_in[slot]

        copies[4].wait()
        copies[5].wait()
        grads_out[...] = quarter_terms(
            place_ref, 1, rating_out, weight_out, users_out, items_out, high_out, low_out
        )
        for copy in copies[6:]:
            copy.wait()

    part_outs = [(square, bf16)] * 2 + [((quarter, rank), f32)]
    rating_0, weight_0, users_0, items_0, noise_0, *errors_1, to_sibling = call(
        first,
        [(dense, bf16)] * 2 + [(users.shape, f32), (items.shape, f32), ((2 * quarter, rank), f32)] + part_outs,
        [place] + tables + [(DISTANT, v) for v in (users, items, noise_items)],
        2 * unit,
        landing + [pltpu.SemaphoreType.DMA((11,))],
    )
    from_sibling_0 = swap(to_sibling, 1)
    stage_0 = [local(rating_0), local(weight_0), local(users_0), local(items_0)]

    def part(flip, place_ref, *refs):
        refs[-1][...] = quarter_terms(place_ref, flip, *refs[:-1])

    def quarter_part(flip, cost, after):
        high, low, grads = call(
            functools.partial(part, flip), part_outs, [place] + stage_0, cost * unit, after=after
        )
        return [high, low], grads

    def join(at, a_ref, b_ref, out):
        out[...] = a_ref[at, :] + b_ref[at, :]

    def add_scaled(at, base_ref, a_ref, out):
        out[...] = base_ref[at, :] + GAIN * a_ref[at, :]

    def rows(k):
        return slice(k * chunk, (k + 1) * chunk)

    def joined(kernel, at, a, b, cost, after):
        return call(
            functools.partial(kernel, at), [(piece, f32)], [local(a), local(b)], cost * unit,
            after=after,
        )

    errors_3, to_sibling = quarter_part(3, COST["part"], [])
    from_sibling_2 = swap(to_sibling, 1)
    errors_0, mine = quarter_part(0, COST["part"], [to_sibling])
    to_chip = []
    for k in range(CHUNKS):
        to_chip += joined(join, rows(k), mine, from_sibling_0, COST["join"], to_chip[-1:])
    from_chip = [swap(value, 2) for value in to_chip]
    errors_2, mine = quarter_part(2, COST["part_2"], to_chip)

    def user_step(place_ref, users_ref, items_ref, noise_ref, *rest):
        errors, users_out = rest[:-1], rest[-1]
        total = jnp.zeros((owned, rank), f32)
        for flip in range(n_grp):
            item_halves = halves(items_ref[rows_of(place_ref, flip), :])
            kept = (errors[2 * flip][...], errors[2 * flip + 1][...])
            total = total + product(kept, item_halves, TN)
        users_out[...] = stepped(users_ref[...], total, noise_ref[0])

    [users_1] = call(
        user_step,
        [(users.shape, f32)],
        [place, local(users_0), local(items_0), local(noise_users)]
        + [local(v) for v in errors_0 + errors_1 + errors_2 + errors_3],
        COST["user_step"] * unit,
    )
    flat = (columns * TILE, owned)

    def layout(place_ref, index_hbm, count_hbm, noise_hbm, rating_ref, weight_ref, users_ref,
               rating_out, weight_out, send_out, noise_out, index_ref, count_ref, sems):
        copies = fetch(
            [(index_hbm, index_ref), (count_hbm, count_ref),
             (noise_hbm.at[1, rows_of(place_ref, 2), :], noise_out)],
            sems,
        )
        rating_out[...] = jnp.zeros_like(rating_out)
        weight_out[...] = jnp.zeros_like(weight_out)
        for copy in copies[:2]:
            copy.wait()
        for slot in range(slots):

            @pl.when(slot < count_ref[1])
            def _(slot=slot):
                tile = index_ref[1, slot]
                at = pl.ds(pl.multiple_of(lax.rem(tile, columns) * TILE, TILE), TILE)
                turned = (rating_ref[1, slot].astype(f32).T, weight_ref[1, slot].astype(f32).T)
                for row in range(owned // TILE):

                    @pl.when(lax.div(tile, columns) == row)
                    def _(row=row):
                        across = slice(row * TILE, (row + 1) * TILE)
                        rating_out[at, across] = turned[0]
                        weight_out[at, across] = turned[1]

        for n, flip in enumerate((1, 3)):
            for offset, values in ((0, rating_out), (2 * quarter, weight_out)):
                at = slice(offset + n * quarter, offset + (n + 1) * quarter)
                send_out[at, :] = values[rows_of(place_ref, flip), :]
        send_out[4 * quarter :, :] = users_ref[...]
        copies[2].wait()

    rating_1, weight_1, to_sibling, noise_1 = call(
        layout,
        [(flat, f32)] * 2 + [((4 * quarter + owned, rank), f32), ((quarter, rank), f32)],
        [place] + tables[:2] + [(DISTANT, noise_items)]
        + [local(v) for v in (ratings, weights, users_1)],
        COST["layout"] * unit,
        landing[:2] + [pltpu.SemaphoreType.DMA((3,))],
        after=[users_1],
    )
    from_sibling = swap(to_sibling, 1)

    def move(n, place_ref, items_ref, noise_ref, own_ref, other_ref, out):
        flip, k = (2, 0)[n // CHUNKS], n % CHUNKS
        start = pl.multiple_of((place_ref[0] ^ flip) * quarter + k * chunk, chunk)
        total = own_ref[...] + other_ref[...]
        out[...] = stepped(items_ref[pl.ds(start, chunk), :], total, noise_ref[rows(n), :])

    def relay(value_ref, out):
        out[...] = value_ref[...]

    def relayed(value, cost, after):
        return call(relay, [(piece, f32)], [local(value)], cost * unit, after=after)

    moved = []
    for n in range(2 * CHUNKS):
        if n < CHUNKS:
            to_chip += joined(
                join, rows(n), mine, from_sibling_2, COST["join_2"],
                [to_sibling, from_chip[n], *moved[-1:]],
            )
        terms = [local(v) for v in (items_0, noise_0, to_chip[(n + CHUNKS) % (2 * CHUNKS)], from_chip[n])]
        moved += call(
            functools.partial(move, n), [(piece, f32)], [place] + terms, COST["move"][n] * unit,
            after=moved[-1:],
        )
        if n < CHUNKS:
            [value] = relayed(to_chip[-1], COST["relay"], moved[-1:])
            from_chip.append(swap(value, 2))
    ahead = [onward(value) for value in moved]

    def late(k, slot, place_ref, items_ref, users_ref, rating_ref, weight_ref, sibling_ref, *rest):
        high_out, low_out, high_s_out, low_s_out, out = rest[-5:]
        own, other = halves(users_ref[...]), halves(sibling_ref[4 * quarter :, :])
        now = items_ref[...]
        item_halves = halves(now)
        at = pl.ds(pl.multiple_of((place_ref[0] ^ (2 * slot)) * quarter + k * chunk, chunk), chunk)
        errors = errors_of(item_halves, own, rating_ref[at, :], weight_ref[at, :])
        high_out[...], low_out[...] = errors
        total = product(errors, own, NN)
        at = slot * quarter + k * chunk
        rating = sibling_ref[at : at + chunk, :]
        weight = sibling_ref[2 * quarter + at : 2 * quarter + at + chunk, :]
        errors = errors_of(item_halves, other, rating, weight)
        high_s_out[...], low_s_out[...] = errors
        total = total + product(errors, other, NN)
        if slot == 1:
            total = stepped(now, total, rest[0][rows(k), :])
        out[...] = total

    common = [local(v) for v in (users_1, rating_1, weight_1, from_sibling)]
    errors_shape = (chunk, owned)
    late_outs = [(errors_shape, bf16)] * 4 + [(piece, f32)]
    here, there = ahead[:CHUNKS], ahead[CHUNKS:]
    errors_here, sent = [], []
    for k in range(CHUNKS):
        *errors, value = call(
            functools.partial(late, k, 0), late_outs, [place, local(here[k])] + common,
            COST["near"][k] * unit, after=sent[-1:],
        )
        errors_here.append(errors)
        sent.append(value)
    received = [swap(value, 2) for value in sent]
    errors_there, finished = [], []
    for k in range(CHUNKS):
        *errors, value = call(
            functools.partial(late, k, 1), late_outs,
            [place, local(there[k])] + common + [local(noise_1)], COST["far"][k] * unit,
            after=[sent[-1], *finished[-1:]],
        )
        errors_there.append(errors)
        finished += joined(add_scaled, rows(0), value, received[k], COST["finish"], [])
    final = [onward(value) for value in finished]

    def stack(*refs):
        for k in range(CHUNKS):
            refs[-1][rows(k), :] = refs[k][...]

    known = [
        local(v)
        for errors, values in zip(errors_here + errors_there, here + there)
        for v in (*errors, values)
    ]
    step = -(-owned // (8 * SHARES)) * 8
    shares_at = [slice(n * step, min((n + 1) * step, owned)) for n in range(SHARES)]

    def user_sums(*refs):
        own = other = jnp.zeros((owned, rank), f32)
        for n in range(2 * CHUNKS):
            high, low, high_s, low_s, values = (ref[...] for ref in refs[5 * n : 5 * n + 5])
            item_halves = halves(values)
            own = own + product((high, low), item_halves, TN)
            other = other + product((high_s, low_s), item_halves, TN)
        refs[10 * CHUNKS][...] = own
        for n, ref in enumerate(refs[10 * CHUNKS + 1 :]):
            ref[...] = other[shares_at[n], :]

    sums, *to_sibling = call(
        user_sums, [(users.shape, f32)] + [((at.stop - at.start, rank), f32) for at in shares_at],
        known, COST["user_sums"] * unit,
        after=finished,
    )
    from_sibling = [swap(value, 1) for value in to_sibling]

    def last(users_ref, sums_ref, noise_ref, *rest):
        shares, (users_out, token) = rest[:SHARES], rest[SHARES:]
        token[...] = jnp.zeros_like(token)
        for at, ref in zip(shares_at, shares):
            total = sums_ref[at, :] + ref[...]
            users_out[at, :] = stepped(users_ref[at, :], total, noise_ref[1, at, :])

    users_out, token = call(
        last,
        [(users.shape, f32), ((8, 128), f32)],
        [local(users_1), local(sums), local(noise_users)] + [local(v) for v in from_sibling],
        COST["last"] * unit,
    )

    [early] = relayed(final[0], COST["final"], [token])
    [items_out] = call(stack, [((quarter, rank), f32)], [local(early), local(final[1])], 1)
    return (users_out, items_out)


def solution(mesh):
    in_specs = (
        P(("blk", "grp"), None),
        P("blk", None),
        P(None, ("blk", "grp"), None),
        P(None, "blk", None),
        P(None, ("blk", "grp")),
        P(None, ("blk", "grp")),
        P(None, ("blk", "grp"), None, None),
        P(None, ("blk", "grp"), None, None),
    )
    out_specs = (P(("blk", "grp"), None), P(("blk", "grp"), None))
    return jax.shard_map(body, mesh=mesh, in_specs=in_specs, out_specs=out_specs, check_vma=False)
```

```python
import functools
import math

import jax
import jax.numpy as jnp
from jax import lax
from jax.experimental import pallas as pl
from jax.experimental.pallas import tpu as pltpu
from jax.sharding import PartitionSpec as P

STEP_SIZE = 0.001
LIKELIHOOD = 20.0
NOISE_SCALE = math.sqrt(0.002)
GAIN = STEP_SIZE * LIKELIHOOD
AXES = ("blk", "grp")
TILE = 128
CHUNKS = 2
SHARES = 3
WEIGHT = 8
COST = {"part": 2, "join": 0, "join_2": 4, "relay": 1, "part_2": 2, "move": (4, 4, 4, 4), "user_step": 0, "layout": 0, "near": (2, 2), "far": (2, 2), "finish": 0, "user_sums": 64, "last": 0, "final": 0}
VMEM_LIMIT = 16 * 1024 * 1024

NN = (((1,), (0,)), ((), ()))
NT = (((1,), (1,)), ((), ()))
TN = (((0,), (0,)), ((), ()))


def halves(value):
    high = value.astype(jnp.bfloat16)
    low = (value - high.astype(jnp.float32)).astype(jnp.bfloat16)
    return high, low


def product(left, right, dims):
    dot = functools.partial(
        lax.dot_general, dimension_numbers=dims, preferred_element_type=jnp.float32
    )
    return dot(left[0], right[0]) + (dot(left[0], right[1]) + dot(left[1], right[0]))


def errors_of(item_halves, user_halves, rating, weight):
    predicted = product(item_halves, user_halves, NT)
    return halves(weight.astype(jnp.float32) * (rating.astype(jnp.float32) - predicted))


def stepped(now, total, noise):
    return now + STEP_SIZE * (LIKELIHOOD * total - now) + NOISE_SCALE * noise


SCALARS = pl.BlockSpec(memory_space=pltpu.SMEM)
LOCAL = pl.BlockSpec(memory_space=pltpu.VMEM)
DISTANT = pl.BlockSpec(memory_space=pltpu.HBM)
AFTER = pl.BlockSpec(memory_space=pl.ANY)


def call(body, outs, operands, cost, scratch=(), after=()):
    unread = len(after)

    def kernel(*refs):
        body(*refs[unread:])

    return pl.pallas_call(
        kernel,
        in_specs=[AFTER] * unread + [spec for spec, _ in operands],
        out_specs=[LOCAL] * len(outs),
        out_shape=[jax.ShapeDtypeStruct(shape, dtype) for shape, dtype in outs],
        scratch_shapes=list(scratch),
        compiler_params=pltpu.CompilerParams(vmem_limit_bytes=VMEM_LIMIT),
        cost_estimate=pl.CostEstimate(
            flops=WEIGHT * cost, bytes_accessed=1 << 18, transcendentals=0
        ),
        name=body.__name__ if hasattr(body, "__name__") else body.func.__name__,
    )(*after, *[held(spec, array) for spec, array in operands])


def held(spec, array):
    return pltpu.with_memory_space_constraint(array, pltpu.HBM) if spec is DISTANT else array


def local(array):
    return (LOCAL, array)


def body(users, items, noise_users, noise_items, tile_index, counts, ratings, weights):
    f32, bf16 = jnp.float32, jnp.bfloat16
    n_blk, n_grp = lax.axis_size("blk"), lax.axis_size("grp")
    owned, rank = users.shape
    slots = ratings.shape[1]
    columns = items.shape[0] // TILE
    per_quarter = columns // n_grp
    quarter = per_quarter * TILE
    chunk = quarter // CHUNKS
    place = (SCALARS, lax.axis_index("grp").astype(jnp.int32).reshape(1))

    def swap(value, other):
        pairs = [
            (b * n_grp + g, b * n_grp + (g ^ other)) for b in range(n_blk) for g in range(n_grp)
        ]
        with jax.named_scope("core_swap" if other == 1 else "chip_swap"):
            return lax.ppermute(value, AXES, pairs)

    def onward(value):
        pairs = [
            (b * n_grp + g, (b + 1) % n_blk * n_grp + (g ^ 2))
            for b in range(n_blk)
            for g in range(n_grp)
        ]
        with jax.named_scope("onward"):
            return lax.ppermute(value, AXES, pairs)

    dense = (columns, owned, TILE)
    piece = (chunk, rank)
    square = (quarter, owned)
    unit = 2 * owned * quarter * rank * 3

    def rows_of(place_ref, flip):
        return pl.ds(pl.multiple_of((place_ref[0] ^ flip) * quarter, quarter), quarter)

    def side_by_side(dense_ref, start):
        return jnp.concatenate([dense_ref[start + t] for t in range(per_quarter)], 1)

    def quarter_terms(place_ref, flip, rating_ref, weight_ref, users_ref, items_ref, high_ref, low_ref):
        start = (place_ref[0] ^ flip) * per_quarter
        user_halves = halves(users_ref[...])
        item_halves = halves(items_ref[rows_of(place_ref, flip), :])
        rating = side_by_side(rating_ref, start).astype(f32).T
        weight = side_by_side(weight_ref, start).astype(f32).T
        errors = errors_of(item_halves, user_halves, rating, weight)
        high_ref[...], low_ref[...] = errors
        return product(errors, user_halves, NN)

    def fetch(pairs, sems):
        copies = [pltpu.make_async_copy(a, b, sems.at[n]) for n, (a, b) in enumerate(pairs)]
        for copy in copies:
            copy.start()
        return copies

    live = counts.reshape(-1)
    tables = [(DISTANT, tile_index), (DISTANT, live), (DISTANT, ratings), (DISTANT, weights)]
    landing = [
        pltpu.SMEM(tile_index.shape, jnp.int32),
        pltpu.SMEM(live.shape, jnp.int32),
        pltpu.VMEM(ratings.shape[1:], bf16),
        pltpu.VMEM(weights.shape[1:], bf16),
    ]

    def first(place_ref, index_hbm, count_hbm, rating_hbm, weight_hbm, users_hbm, items_hbm, noise_hbm,
              rating_out, weight_out, users_out, items_out, noise_out, high_out, low_out, grads_out,
              index_ref, count_ref, rating_in, weight_in, sems):
        copies = fetch(
            [(index_hbm, index_ref), (count_hbm, count_ref),
             (rating_hbm.at[0], rating_in), (weight_hbm.at[0], weight_in), (users_hbm, users_out)]
            + [(items_hbm.at[rows_of(place_ref, flip), :], items_out.at[rows_of(place_ref, flip), :])
               for flip in (1, 0, 3, 2)]
            + [(noise_hbm.at[0, rows_of(place_ref, 2), :], noise_out.at[:quarter, :]),
               (noise_hbm.at[0, rows_of(place_ref, 0), :], noise_out.at[quarter:, :])],
            sems,
        )
        rating_out[...] = jnp.zeros_like(rating_out)
        weight_out[...] = jnp.zeros_like(weight_out)
        for copy in copies[:4]:
            copy.wait()
        for slot in range(slots):

            @pl.when(slot < count_ref[0])
            def _(slot=slot):
                tile = index_ref[0, slot]
                column = lax.rem(tile, columns)
                row = pl.multiple_of(lax.div(tile, columns) * TILE, TILE)
                rating_out[column, pl.ds(row, TILE), :] = rating_in[slot]
                weight_out[column, pl.ds(row, TILE), :] = weight_in[slot]

        copies[4].wait()
        copies[5].wait()
        grads_out[...] = quarter_terms(
            place_ref, 1, rating_out, weight_out, users_out, items_out, high_out, low_out
        )
        for copy in copies[6:]:
            copy.wait()

    part_outs = [(square, bf16)] * 2 + [((quarter, rank), f32)]
    rating_0, weight_0, users_0, items_0, noise_0, *errors_1, to_sibling = call(
        first,
        [(dense, bf16)] * 2 + [(users.shape, f32), (items.shape, f32), ((2 * quarter, rank), f32)] + part_outs,
        [place] + tables + [(DISTANT, v) for v in (users, items, noise_items)],
        2 * unit,
        landing + [pltpu.SemaphoreType.DMA((11,))],
    )
    from_sibling_0 = swap(to_sibling, 1)
    stage_0 = [local(rating_0), local(weight_0), local(users_0), local(items_0)]

    def part(flip, place_ref, *refs):
        refs[-1][...] = quarter_terms(place_ref, flip, *refs[:-1])

    def quarter_part(flip, cost, after):
        high, low, grads = call(
            functools.partial(part, flip), part_outs, [place] + stage_0, cost * unit, after=after
        )
        return [high, low], grads

    def join(at, a_ref, b_ref, out):
        out[...] = a_ref[at, :] + b_ref[at, :]

    def add_scaled(at, base_ref, a_ref, out):
        out[...] = base_ref[at, :] + GAIN * a_ref[at, :]

    def rows(k):
        return slice(k * chunk, (k + 1) * chunk)

    def joined(kernel, at, a, b, cost, after):
        return call(
            functools.partial(kernel, at), [(piece, f32)], [local(a), local(b)], cost * unit,
            after=after,
        )

    errors_3, to_sibling = quarter_part(3, COST["part"], [])
    from_sibling_2 = swap(to_sibling, 1)
    errors_0, mine = quarter_part(0, COST["part"], [to_sibling])
    to_chip = []
    for k in range(CHUNKS):
        to_chip += joined(join, rows(k), mine, from_sibling_0, COST["join"], to_chip[-1:])
    from_chip = [swap(value, 2) for value in to_chip]
    errors_2, mine = quarter_part(2, COST["part_2"], to_chip)

    def user_step(place_ref, users_ref, items_ref, noise_ref, *rest):
        errors, users_out = rest[:-1], rest[-1]
        total = jnp.zeros((owned, rank), f32)
        for flip in range(n_grp):
            item_halves = halves(items_ref[rows_of(place_ref, flip), :])
            kept = (errors[2 * flip][...], errors[2 * flip + 1][...])
            total = total + product(kept, item_halves, TN)
        users_out[...] = stepped(users_ref[...], total, noise_ref[0])

    [users_1] = call(
        user_step,
        [(users.shape, f32)],
        [place, local(users_0), local(items_0), local(noise_users)]
        + [local(v) for v in errors_0 + errors_1 + errors_2 + errors_3],
        COST["user_step"] * unit,
    )
    flat = (columns * TILE, owned)

    def layout(place_ref, index_hbm, count_hbm, noise_hbm, rating_ref, weight_ref, users_ref,
               rating_out, weight_out, send_out, noise_out, index_ref, count_ref, sems):
        copies = fetch(
            [(index_hbm, index_ref), (count_hbm, count_ref),
             (noise_hbm.at[1, rows_of(place_ref, 2), :], noise_out)],
            sems,
        )
        rating_out[...] = jnp.zeros_like(rating_out)
        weight_out[...] = jnp.zeros_like(weight_out)
        for copy in copies[:2]:
            copy.wait()
        for slot in range(slots):

            @pl.when(slot < count_ref[1])
            def _(slot=slot):
                tile = index_ref[1, slot]
                at = pl.ds(pl.multiple_of(lax.rem(tile, columns) * TILE, TILE), TILE)
                turned = (rating_ref[1, slot].astype(f32).T, weight_ref[1, slot].astype(f32).T)
                for row in range(owned // TILE):

                    @pl.when(lax.div(tile, columns) == row)
                    def _(row=row):
                        across = slice(row * TILE, (row + 1) * TILE)
                        rating_out[at, across] = turned[0]
                        weight_out[at, across] = turned[1]

        for n, flip in enumerate((1, 3)):
            for offset, values in ((0, rating_out), (2 * quarter, weight_out)):
                at = slice(offset + n * quarter, offset + (n + 1) * quarter)
                send_out[at, :] = values[rows_of(place_ref, flip), :]
        send_out[4 * quarter :, :] = users_ref[...]
        copies[2].wait()

    rating_1, weight_1, to_sibling, noise_1 = call(
        layout,
        [(flat, f32)] * 2 + [((4 * quarter + owned, rank), f32), ((quarter, rank), f32)],
        [place] + tables[:2] + [(DISTANT, noise_items)]
        + [local(v) for v in (ratings, weights, users_1)],
        COST["layout"] * unit,
        landing[:2] + [pltpu.SemaphoreType.DMA((3,))],
        after=[users_1],
    )
    from_sibling = swap(to_sibling, 1)

    def move(n, place_ref, items_ref, noise_ref, own_ref, other_ref, out):
        flip, k = (2, 0)[n // CHUNKS], n % CHUNKS
        start = pl.multiple_of((place_ref[0] ^ flip) * quarter + k * chunk, chunk)
        total = own_ref[...] + other_ref[...]
        out[...] = stepped(items_ref[pl.ds(start, chunk), :], total, noise_ref[rows(n), :])

    def relay(value_ref, out):
        out[...] = value_ref[...]

    def relayed(value, cost, after):
        return call(relay, [(piece, f32)], [local(value)], cost * unit, after=after)

    moved = []
    for n in range(2 * CHUNKS):
        if n < CHUNKS:
            to_chip += joined(
                join, rows(n), mine, from_sibling_2, COST["join_2"],
                [to_sibling, from_chip[n], *moved[-1:]],
            )
        terms = [local(v) for v in (items_0, noise_0, to_chip[(n + CHUNKS) % (2 * CHUNKS)], from_chip[n])]
        moved += call(
            functools.partial(move, n), [(piece, f32)], [place] + terms, COST["move"][n] * unit,
            after=moved[-1:],
        )
        if n < CHUNKS:
            [value] = relayed(to_chip[-1], COST["relay"], moved[-1:])
            from_chip.append(swap(value, 2))
    ahead = [onward(value) for value in moved]

    def late(k, slot, place_ref, items_ref, users_ref, rating_ref, weight_ref, sibling_ref, *rest):
        high_out, low_out, high_s_out, low_s_out, out = rest[-5:]
        both = halves(jnp.concatenate([users_ref[...], sibling_ref[4 * quarter :, :]], 0))
        now = items_ref[...]
        item_halves = halves(now)
        at = pl.ds(pl.multiple_of((place_ref[0] ^ (2 * slot)) * quarter + k * chunk, chunk), chunk)
        there_at = slice(slot * quarter + k * chunk, slot * quarter + (k + 1) * chunk)
        weights_at = slice(2 * quarter + there_at.start, 2 * quarter + there_at.stop)
        rating = jnp.concatenate([rating_ref[at, :], sibling_ref[there_at, :]], 1)
        weight = jnp.concatenate([weight_ref[at, :], sibling_ref[weights_at, :]], 1)
        high, low = errors_of(item_halves, both, rating, weight)
        high_out[...], low_out[...] = high[:, :owned], low[:, :owned]
        high_s_out[...], low_s_out[...] = high[:, owned:], low[:, owned:]
        total = product((high, low), both, NN)
        if slot == 1:
            total = stepped(now, total, rest[0][rows(k), :])
        out[...] = total

    common = [local(v) for v in (users_1, rating_1, weight_1, from_sibling)]
    errors_shape = (chunk, owned)
    late_outs = [(errors_shape, bf16)] * 4 + [(piece, f32)]
    here, there = ahead[:CHUNKS], ahead[CHUNKS:]
    errors_here, sent = [], []
    for k in range(CHUNKS):
        *errors, value = call(
            functools.partial(late, k, 0), late_outs, [place, local(here[k])] + common,
            COST["near"][k] * unit, after=sent[-1:],
        )
        errors_here.append(errors)
        sent.append(value)
    received = [swap(value, 2) for value in sent]
    errors_there, finished = [], []
    for k in range(CHUNKS):
        *errors, value = call(
            functools.partial(late, k, 1), late_outs,
            [place, local(there[k])] + common + [local(noise_1)], COST["far"][k] * unit,
            after=[sent[-1], *finished[-1:]],
        )
        errors_there.append(errors)
        finished += joined(add_scaled, rows(0), value, received[k], COST["finish"], [])
    final = [onward(value) for value in finished]

    def stack(*refs):
        for k in range(CHUNKS):
            refs[-1][rows(k), :] = refs[k][...]

    known = [
        local(v)
        for errors, values in zip(errors_here + errors_there, here + there)
        for v in (*errors, values)
    ]
    step = -(-owned // (8 * SHARES)) * 8
    shares_at = [slice(n * step, min((n + 1) * step, owned)) for n in range(SHARES)]

    def user_sums(*refs):
        own = other = jnp.zeros((owned, rank), f32)
        for n in range(2 * CHUNKS):
            high, low, high_s, low_s, values = (ref[...] for ref in refs[5 * n : 5 * n + 5])
            item_halves = halves(values)
            own = own + product((high, low), item_halves, TN)
            other = other + product((high_s, low_s), item_halves, TN)
        refs[10 * CHUNKS][...] = own
        for n, ref in enumerate(refs[10 * CHUNKS + 1 :]):
            ref[...] = other[shares_at[n], :]

    sums, *to_sibling = call(
        user_sums, [(users.shape, f32)] + [((at.stop - at.start, rank), f32) for at in shares_at],
        known, COST["user_sums"] * unit,
        after=finished,
    )
    from_sibling = [swap(value, 1) for value in to_sibling]

    def last(users_ref, sums_ref, noise_ref, *rest):
        shares, (users_out, token) = rest[:SHARES], rest[SHARES:]
        token[...] = jnp.zeros_like(token)
        for at, ref in zip(shares_at, shares):
            total = sums_ref[at, :] + ref[...]
            users_out[at, :] = stepped(users_ref[at, :], total, noise_ref[1, at, :])

    users_out, token = call(
        last,
        [(users.shape, f32), ((8, 128), f32)],
        [local(users_1), local(sums), local(noise_users)] + [local(v) for v in from_sibling],
        COST["last"] * unit,
    )

    [early] = relayed(final[0], COST["final"], [token])
    [items_out] = call(stack, [((quarter, rank), f32)], [local(early), local(final[1])], 1)
    return (users_out, items_out)


def solution(mesh):
    in_specs = (
        P(("blk", "grp"), None),
        P("blk", None),
        P(None, ("blk", "grp"), None),
        P(None, "blk", None),
        P(None, ("blk", "grp")),
        P(None, ("blk", "grp")),
        P(None, ("blk", "grp"), None, None),
        P(None, ("blk", "grp"), None, None),
    )
    out_specs = (P(("blk", "grp"), None), P(("blk", "grp"), None))
    return jax.shard_map(body, mesh=mesh, in_specs=in_specs, out_specs=out_specs, check_vma=False)
```
